128 devices in a mesh: section: 8 (over z_lo, x), fsdp: 16 (over y, z_hi, core).
Axes of the slice: x: 4, y: 4, z: 4 (z_hi: 2, z_lo: 2; z = z_hi * 2 + z_lo), core: 2. Of those that a mesh axis runs over, the one named last changes fastest.
Arguments:
- in_base: bfloat16 [8, 5, 768, 9216], P('section', None, 'fsdp'), may hold values from -5 to 5
- out_base: bfloat16 [8, 5, 768, 9216], P('section', None, 'fsdp'), may hold values from -5 to 5, as said below
- sample_ids: int32 [4], replicated, may hold values from 0 to 4, as said below
- send_exponent: int32 [8, 4, 768, 72], P('section', None, 'fsdp'), may hold values from -9 to -4
- grad_exponent: int32 [8, 4, 768, 72], P('section', None, 'fsdp'), may hold values from -9 to -4
- loss_grad: bfloat16 [4, 768, 9216], P(None, 'fsdp'), may hold values from -6 to 6
- down_weight: bfloat16 [8, 9216, 256], P('section', 'fsdp'), may hold values from -0.0625 to 0.0625
- up_weight: bfloat16 [8, 9216, 256], P('section', 'fsdp'), may hold values from -0.0625 to 0.0625
- norm_gain: bfloat16 [8, 9216], P('section', 'fsdp'), may hold values from 0.5 to 2
Outputs:
- section_out: bfloat16 [8, 4, 768, 9216], P('section', None, 'fsdp')
- input_grad: bfloat16 [8, 4, 768, 9216], P('section', None, 'fsdp')
- down_grad: float32 [8, 9216, 256], P('section', 'fsdp')
- up_grad: float32 [8, 9216, 256], P('section', 'fsdp')
- gain_grad: float32 [8, 9216], P('section', 'fsdp')
The draws below stay inside these ranges and needn't reach their ends.
Inputs may be any that keep to these rules, and one draw needn't show every extreme that they name: `sample_ids`: 4 different samples; 0 and 4 are among them. out_base[s] equals in_base[s + 1] for s < 7.
All inputs are finite; a program needn't handle non-finite values.
Results may differ from the reference program's by a relative error of at most 0.025.
Values may be sent and summed in bfloat16 or wider, within the bound.
No kernel may reach another device: no remote copies, remote signals or barrier semaphores. Data moves between devices by JAX's collectives and lax.ppermute only.
A program may use at most 128 MiB of HBM per device.

```python
import math
import jax
import jax.numpy as jnp
from jax import lax

HIDDEN_DIMENSION = 9216
RANK = 256
MICRO = 4
EXAMPLE_POOL = 5
TOK_MB = 48
SECTIONS = 8
BATCHLET_ITEMS = 768
BLOCKS = 72
N_FSDP = 16


def stored_chain(key):
    current = jax.random.truncated_normal(jax.random.fold_in(key, 100), -4.0, 4.0, (EXAMPLE_POOL, BATCHLET_ITEMS, HIDDEN_DIMENSION), jnp.float32)
    layers = [current.astype(jnp.bfloat16)]
    for index in range(SECTIONS):
        iteration_seed = jax.random.fold_in(key, 200 + index)
        noise = jax.random.truncated_normal(jax.random.fold_in(iteration_seed, 1), -4.0, 4.0, (EXAMPLE_POOL, BATCHLET_ITEMS, HIDDEN_DIMENSION), jnp.float32)
        spike_tallies = jax.random.uniform(jax.random.fold_in(iteration_seed, 2), (EXAMPLE_POOL, BATCHLET_ITEMS, HIDDEN_DIMENSION // 128, 1), jnp.float32)
        difference_scaling = jnp.where(spike_tallies < 0.0625, 20.0, 1.0)
        noise = (noise.reshape(EXAMPLE_POOL, BATCHLET_ITEMS, HIDDEN_DIMENSION // 128, 128) * difference_scaling).reshape(EXAMPLE_POOL, BATCHLET_ITEMS, HIDDEN_DIMENSION) * 0.05
        current = jnp.clip(current + noise, -5.0, 5.0)
        layers.append(current.astype(jnp.bfloat16))
    return layers


def draw_in_base(key, part):
    return jnp.stack(stored_chain(key)[:SECTIONS])


def draw_out_base(key, part):
    return jnp.stack(stored_chain(key)[1:])


def draw_sample_ids(key, part):
    key = jax.random.fold_in(key, 7919)
    middle = jax.random.permutation(jax.random.fold_in(key, 1), EXAMPLE_POOL - 2)[:MICRO - 2].astype(jnp.int32) + 1
    chosen = jnp.concatenate([jnp.array([0, EXAMPLE_POOL - 1], jnp.int32), middle])
    order = jax.random.permutation(jax.random.fold_in(key, 2), MICRO)
    return chosen[order].astype(jnp.int32)


def touch_ends(result, rng, least, top_value):
    longest = result.shape.index(max(result.shape))
    spots = []
    for shift in (0, 1):
        where = [jax.random.randint(jax.random.fold_in(rng, axis), (), 0, length) for axis, length in enumerate(result.shape)]
        where[longest] = (where[longest] + shift) % result.shape[longest]
        spots.append(tuple(where))
    return result.at[spots[0]].set(least).at[spots[1]].set(top_value)


def steps_of(key, dims, cuts, smallest, largest):
    level = 1.0
    for axis_at, parts in cuts:
        draws = jax.random.uniform(jax.random.fold_in(jax.random.fold_in(key, 6), axis_at), (parts,), jnp.float32, smallest / len(cuts), largest / len(cuts))
        level = level * jnp.repeat(jnp.exp(draws), dims[axis_at] // parts).reshape((-1,) + (1,) * (len(dims) - 1 - axis_at))
    return level


def bell_draw(stream_key, dims, scale, bound, split=(), dtype=jnp.bfloat16):
    values = scale * jax.random.normal(stream_key, dims, jnp.float32)
    if split:
        values = values * steps_of(stream_key, dims, split, -0.22, 0.18)
    return jnp.clip(values, -bound, bound).astype(dtype)


def setup_inputs(seed: int = 0) -> dict:
    keys = jax.random.split(jax.random.key(seed), 10)
    in_base = draw_in_base(jax.random.fold_in(keys[9], 71), 0)
    out_base = draw_out_base(jax.random.fold_in(keys[9], 71), 0)
    sample_ids = draw_sample_ids(jax.random.fold_in(keys[9], 71), 0)
    send_exponent = touch_ends(jax.random.randint(keys[3], (SECTIONS, MICRO, BATCHLET_ITEMS, BLOCKS), -9, -3), jax.random.fold_in(keys[3], 1), -9, (-3) - 1).astype(jnp.int32)
    grad_exponent = touch_ends(jax.random.randint(keys[4], (SECTIONS, MICRO, BATCHLET_ITEMS, BLOCKS), -9, -3), jax.random.fold_in(keys[4], 1), -9, (-3) - 1).astype(jnp.int32)
    loss_grad = bell_draw(keys[5], (MICRO, BATCHLET_ITEMS, HIDDEN_DIMENSION), 1.0, 6.0, ((1, 16),))
    down_weight = bell_draw(keys[6], (SECTIONS, HIDDEN_DIMENSION, RANK), HIDDEN_DIMENSION ** -0.5, 0.0625, ((0, 8), (1, 16)))
    up_weight = bell_draw(keys[7], (SECTIONS, HIDDEN_DIMENSION, RANK), HIDDEN_DIMENSION ** -0.5, 0.0625, ((0, 8), (1, 16)))
    norm_gain = jnp.clip(jnp.exp(math.log(2.0) - 1.3862944 * jax.random.uniform(keys[8], (SECTIONS, HIDDEN_DIMENSION), jnp.float32) ** steps_of(keys[8], (SECTIONS, HIDDEN_DIMENSION), ((0, 8), (1, 16)), -0.2, 0.2)), 0.5, 2.0).astype(jnp.bfloat16)
    return dict(in_base=in_base, out_base=out_base, sample_ids=sample_ids, send_exponent=send_exponent, grad_exponent=grad_exponent, loss_grad=loss_grad, down_weight=down_weight, up_weight=up_weight, norm_gain=norm_gain)


SQRT_HALF = 0.7071067811865476
INV_ROOT_TAU = 0.3989422804014327
clip_level = 448.0
norm_epsilon = 1e-05
lowest_exponent = -9
highest_exponent = -3

def gelu_value(values):
    return values * 0.5 * (1.0 + lax.erf(values * SQRT_HALF))

def gelu_slope(values):
    return 0.5 * (1.0 + lax.erf(values * SQRT_HALF)) + values * INV_ROOT_TAU * jnp.exp(-0.5 * values * values)

def block_powers(exponent):
    upward = jnp.zeros(exponent.shape, jnp.float32)
    downward = jnp.zeros(exponent.shape, jnp.float32)
    for exponent_value in range(lowest_exponent, highest_exponent):
        matches = exponent == exponent_value
        upward = jnp.where(matches, jnp.float32(2.0 ** exponent_value), upward)
        downward = jnp.where(matches, jnp.float32(2.0 ** (-exponent_value)), downward)
    return (upward, downward)

def encode(values, exponent):
    upward, downward = block_powers(exponent)
    full_shape = values.shape
    layer_groups = values.reshape(full_shape[:-1] + (full_shape[-1] // 128, 128))
    scaled = jnp.clip(layer_groups * downward[..., None], -clip_level, clip_level).astype(jnp.bfloat16)
    scaled = lax.optimization_barrier(scaled)
    return (scaled.astype(jnp.float32) * upward[..., None]).astype(jnp.bfloat16).reshape(full_shape)

def normalize(layer_in):
    values = layer_in.astype(jnp.float32)
    centred = values - lax.optimization_barrier(jnp.mean(values, axis=-1, keepdims=True))
    inv_scale = lax.rsqrt(lax.optimization_barrier(jnp.mean(centred * centred, axis=-1, keepdims=True)) + norm_epsilon)
    return (centred * inv_scale, inv_scale)

def section_forward(layer_in, gain, down_mat, up_mat):
    centred, inv_scale = normalize(layer_in)
    normed = (centred * gain.astype(jnp.float32)).astype(jnp.bfloat16)
    bottleneck = jnp.einsum('mrd,dk->mrk', normed.astype(jnp.float32), down_mat.astype(jnp.float32))
    activated = gelu_value(bottleneck).astype(jnp.bfloat16)
    branch = jnp.einsum('mrk,dk->mrd', activated.astype(jnp.float32), up_mat.astype(jnp.float32))
    section_val = (layer_in.astype(jnp.float32) + branch).astype(jnp.bfloat16)
    return (centred, inv_scale, normed, bottleneck, activated, section_val)

def group_rows(values):
    return values.reshape(values.shape[0], N_FSDP, TOK_MB, values.shape[-1])

def reduce_groups(partials, factor):
    rounded = lax.optimization_barrier((partials * factor).astype(jnp.bfloat16))
    return lax.optimization_barrier(jnp.sum(rounded.astype(jnp.float32), axis=0))

def reference(in_base, out_base, sample_ids, send_exponent, grad_exponent, loss_grad, down_weight, up_weight, norm_gain):
    sections = in_base.shape[0]
    factor = 1.0 / math.sqrt(MICRO * BATCHLET_ITEMS)
    outputs = []
    inputs = []
    delivered = None
    for section_no in range(sections):
        base_rows = in_base[section_no][sample_ids]
        if section_no == 0:
            layer_in = base_rows
        else:
            layer_in = (base_rows.astype(jnp.float32) + delivered.astype(jnp.float32)).astype(jnp.bfloat16)
        inputs.append(layer_in)
        section_val = section_forward(layer_in, norm_gain[section_no], down_weight[section_no], up_weight[section_no])[5]
        outputs.append(section_val)
        if section_no < sections - 1:
            stored = out_base[section_no][sample_ids]
            delivered = encode(section_val.astype(jnp.float32) - stored.astype(jnp.float32), send_exponent[section_no])
    out_cot = loss_grad
    in_grads = [None] * sections
    downs = [None] * sections
    ups = [None] * sections
    gains = [None] * sections
    for section_no in reversed(range(sections)):
        gain = norm_gain[section_no].astype(jnp.float32)
        centred, inv_scale, normed, bottleneck, activated, unused_out = section_forward(inputs[section_no], norm_gain[section_no], down_weight[section_no], up_weight[section_no])
        up_mat = up_weight[section_no].astype(jnp.float32)
        down_mat = down_weight[section_no].astype(jnp.float32)
        act_cot = jnp.einsum('mrd,dk->mrk', out_cot.astype(jnp.float32), up_mat)
        neck_cot = (act_cot * gelu_slope(bottleneck)).astype(jnp.bfloat16)
        norm_cot = jnp.einsum('mrk,dk->mrd', neck_cot.astype(jnp.float32), down_mat)
        scaled_cot = norm_cot * gain
        in_cot = out_cot.astype(jnp.float32) + inv_scale * (scaled_cot - lax.optimization_barrier(jnp.mean(scaled_cot, axis=-1, keepdims=True)) - centred * lax.optimization_barrier(jnp.mean(scaled_cot * centred, axis=-1, keepdims=True)))
        in_grads[section_no] = in_cot.astype(jnp.bfloat16)
        downs[section_no] = reduce_groups(jnp.einsum('mgta,mgtb->gab', group_rows(normed.astype(jnp.float32)), group_rows(neck_cot.astype(jnp.float32))), factor)
        ups[section_no] = reduce_groups(jnp.einsum('mgta,mgtb->gab', group_rows(out_cot.astype(jnp.float32)), group_rows(activated.astype(jnp.float32))), factor)
        gains[section_no] = reduce_groups(jnp.einsum('mgtd->gd', group_rows(norm_cot * centred)), factor)
        if section_no > 0:
            out_cot = encode(in_cot, grad_exponent[section_no])
    return (jnp.stack(outputs), jnp.stack(in_grads), jnp.stack(downs), jnp.stack(ups), jnp.stack(gains))
```

```python
import functools
import math

import jax
import jax.numpy as jnp
from jax import lax
from jax.experimental import pallas as pl
from jax.experimental.pallas import tpu as pltpu
from jax.sharding import PartitionSpec as P

SQRT_HALF = 0.7071067811865476
INV_ROOT_TAU = 0.3989422804014327
CLIP_LEVEL = 448.0
NORM_EPSILON = 1e-05
LOWEST_EXPONENT = -9
HIGHEST_EXPONENT = -3

SECTIONS = 8
WIDTH = 9216
NECK = 256
BLOCK = 128
TOKENS = 48
MICRO = 4
ROWS = 16
CHUNKS = MICRO * TOKENS // ROWS
SHARD = 576
EXTRA = 16
WIDE = 1024
MEDIUM = 512

VM = pl.BlockSpec(memory_space=pltpu.VMEM)
SM = pl.BlockSpec(memory_space=pltpu.SMEM)
ANY = pl.BlockSpec(memory_space=pl.ANY)
NT = (((1,), (1,)), ((), ()))
TN = (((0,), (0,)), ((), ()))
F32 = jnp.float32
BF16 = jnp.bfloat16


def lane_sum(values):
    return jnp.sum(values, axis=-1, keepdims=True)


def clipped(values, limits, start):
    pieces = []
    for offset in range(0, values.shape[1], BLOCK):
        index = (start + offset) // BLOCK
        bound = jnp.broadcast_to(limits[:, index : index + 1], (values.shape[0], BLOCK))
        pieces.append(jnp.clip(values[:, offset : offset + BLOCK], -bound, bound))
    return jnp.concatenate(pieces, axis=1).astype(BF16)


def forward_kernel(
    tick,
    table,
    incoming,
    gain,
    down,
    up,
    base_in,
    base_out,
    limits,
    *refs,
):
    (outs, scratch) = (refs[6:13], refs[13:])
    layer_all, out_all, neck_all, act_all, normed_all, stat_all, delivered = outs
    rows_in, rows_out, bound, layer, section, neck, act, normed, stat, sems = scratch

    @pl.when(table[tick, 0] == 1)
    def _():
        row = pl.multiple_of(table[tick, 1], ROWS)
        base = pl.multiple_of(table[tick, 2], ROWS)
        here = pl.ds(row, ROWS)
        loads = [
            pltpu.make_async_copy(base_in.at[pl.ds(base, ROWS), :], rows_in, sems.at[0]),
            pltpu.make_async_copy(base_out.at[pl.ds(base, ROWS), :], rows_out, sems.at[1]),
            pltpu.make_async_copy(limits.at[here, :], bound, sems.at[2]),
        ]
        for copy in loads:
            copy.start()
        stores = [
            pltpu.make_async_copy(source, target.at[here, :], sems.at[3 + number])
            for number, (source, target) in enumerate(
                (
                    (layer, layer_all),
                    (section, out_all),
                    (neck, neck_all),
                    (act, act_all),
                    (normed, normed_all),
                    (stat, stat_all),
                )
            )
        ]
        loads[0].wait()
        total = jnp.zeros((ROWS, BLOCK), F32)
        for start in range(0, WIDTH, WIDE):
            span = slice(start, start + WIDE)
            values = (rows_in[:, span].astype(F32) + incoming[:, span].astype(F32)).astype(BF16)
            layer[:, span] = values
            values = values.astype(F32)
            for offset in range(0, WIDE, BLOCK):
                total += values[:, offset : offset + BLOCK]
        stores[0].start()
        mean = lane_sum(total) * (1.0 / WIDTH)
        total = jnp.zeros((ROWS, BLOCK), F32)
        for start in range(0, WIDTH, WIDE):
            values = layer[:, start : start + WIDE].astype(F32) - mean
            values = values * values
            for offset in range(0, WIDE, BLOCK):
                total += values[:, offset : offset + BLOCK]
        scale = lax.rsqrt(lane_sum(total) * (1.0 / WIDTH) + NORM_EPSILON)
        stat[:, :BLOCK] = jnp.broadcast_to(mean, (ROWS, BLOCK))
        stat[:, BLOCK:] = jnp.broadcast_to(scale, (ROWS, BLOCK))
        stores[5].start()
        result = jnp.zeros((ROWS, NECK), F32)
        for start in range(0, WIDTH, WIDE):
            span = slice(start, start + WIDE)
            values = (layer[:, span].astype(F32) - mean) * scale
            values = (values * gain[:, span]).astype(BF16)
            normed[:, span] = values
            result += jnp.dot(values, down[span, :], preferred_element_type=F32)
        stores[4].start()
        neck[...] = result
        stores[2].start()
        activated = (result * 0.5 * (1.0 + lax.erf(result * SQRT_HALF))).astype(BF16)
        act[...] = activated
        stores[3].start()
        loads[1].wait()
        loads[2].wait()
        edges = bound[...]
        for start in range(0, WIDTH, MEDIUM):
            span = slice(start, start + MEDIUM)
            branch = lax.dot_general(activated, up[span, :], NT, preferred_element_type=F32)
            value = (layer[:, span].astype(F32) + branch).astype(BF16)
            section[:, span] = value
            change = value.astype(F32) - rows_out[:, span].astype(F32)
            delivered[:, span] = clipped(change, edges, start)
        stores[1].start()
        for copy in stores:
            copy.wait()


def backward_kernel(
    tick,
    table,
    incoming,
    gain,
    down,
    up,
    loss_grad,
    limits,
    layer_all,
    neck_all,
    stat_all,
    *refs,
):
    (outs, scratch) = (refs[4:12], refs[12:])
    grad_all, cot_all, neckcot_all, gain_all, sent = outs[3:]
    cot, bound, layer, neck, stat, grad, neckcot, gains, hold, sems = scratch

    @pl.when(table[tick, 3] == 1)
    def _():
        row = pl.multiple_of(table[tick, 4], ROWS)
        here = pl.ds(row, ROWS)
        last = table[tick, 5] == 1
        loads = [
            pltpu.make_async_copy(limits.at[here, :], bound, sems.at[0]),
            pltpu.make_async_copy(layer_all.at[here, :], layer, sems.at[1]),
            pltpu.make_async_copy(neck_all.at[here, :], neck, sems.at[2]),
            pltpu.make_async_copy(stat_all.at[here, :], stat, sems.at[3]),
        ]
        for copy in loads:
            copy.start()
        stores = [
            pltpu.make_async_copy(grad, grad_all.at[here, :], sems.at[4]),
            pltpu.make_async_copy(cot, cot_all.at[here, :], sems.at[5]),
            pltpu.make_async_copy(neckcot, neckcot_all.at[here, :], sems.at[6]),
            pltpu.make_async_copy(
                gains, gain_all.at[pl.ds(pl.multiple_of(row // 2, 8), 8), :], sems.at[7]
            ),
        ]

        @pl.when(last)
        def _():
            fetch = pltpu.make_async_copy(loss_grad.at[here, :], cot, sems.at[8])
            fetch.start()
            fetch.wait()

        @pl.when(jnp.logical_not(last))
        def _():
            cot[...] = incoming[...]

        stores[1].start()
        result = jnp.zeros((ROWS, NECK), F32)
        for start in range(0, WIDTH, WIDE):
            span = slice(start, start + WIDE)
            result += jnp.dot(cot[:, span], up[span, :], preferred_element_type=F32)
        loads[2].wait()
        bottle = neck[...]
        slope = 0.5 * (1.0 + lax.erf(bottle * SQRT_HALF)) + bottle * INV_ROOT_TAU * jnp.exp(
            -0.5 * bottle * bottle
        )
        small = (result * slope).astype(BF16)
        neckcot[...] = small
        stores[2].start()
        loads[1].wait()
        loads[3].wait()
        mean = stat[:, :1]
        scale = stat[:, BLOCK : BLOCK + 1]
        first = jnp.zeros((ROWS, BLOCK), F32)
        second = jnp.zeros((ROWS, BLOCK), F32)
        for start in range(0, WIDTH, MEDIUM):
            span = slice(start, start + MEDIUM)
            wide = lax.dot_general(small, down[span, :], NT, preferred_element_type=F32)
            centred = (layer[:, span].astype(F32) - mean) * scale
            product = wide * centred
            gains[:, span] = product[:8, :] + product[8:, :]
            scaled = wide * gain[:, span]
            hold[:, span] = scaled
            product = scaled * centred
            for offset in range(0, MEDIUM, BLOCK):
                first += scaled[:, offset : offset + BLOCK]
                second += product[:, offset : offset + BLOCK]
        stores[3].start()
        first = lane_sum(first) * (1.0 / WIDTH)
        second = lane_sum(second) * (1.0 / WIDTH)
        loads[0].wait()
        edges = bound[...]
        for start in range(0, WIDTH, MEDIUM):
            span = slice(start, start + MEDIUM)
            centred = (layer[:, span].astype(F32) - mean) * scale
            value = cot[:, span].astype(F32) + scale * (hold[:, span] - first - centred * second)
            grad[:, span] = value.astype(BF16)
            sent[:, span] = clipped(value, edges, start)
        stores[0].start()
        for copy in stores:
            copy.wait()


def call_params(megabytes):
    return pltpu.CompilerParams(vmem_limit_bytes=megabytes << 20)


def forward_call(tick, table, incoming, gain, down, up, base_in, base_out, limits, state):
    shape = jax.ShapeDtypeStruct
    outs = [shape(item.shape, item.dtype) for item in state] + [shape((ROWS, WIDTH), BF16)]
    got = pl.pallas_call(
        functools.partial(forward_kernel, tick),
        out_shape=outs,
        in_specs=[SM, VM, VM, VM, VM, ANY, ANY, ANY] + [ANY] * 6,
        out_specs=[ANY] * 6 + [VM],
        scratch_shapes=[
            pltpu.VMEM((ROWS, WIDTH), BF16),
            pltpu.VMEM((ROWS, WIDTH), BF16),
            pltpu.VMEM((ROWS, WIDTH // BLOCK), F32),
            pltpu.VMEM((ROWS, WIDTH), BF16),
            pltpu.VMEM((ROWS, WIDTH), BF16),
            pltpu.VMEM((ROWS, NECK), F32),
            pltpu.VMEM((ROWS, NECK), BF16),
            pltpu.VMEM((ROWS, WIDTH), BF16),
            pltpu.VMEM((ROWS, 2 * BLOCK), F32),
            pltpu.SemaphoreType.DMA((9,)),
        ],
        input_output_aliases={8 + number: number for number in range(6)},
        compiler_params=call_params(24),
        cost_estimate=pl.CostEstimate(flops=150_000_000, bytes_accessed=9_000_000, transcendentals=0),
        name="section_forward",
    )(table, incoming, gain, down, up, base_in, base_out, limits, *state)
    return got[:6], got[6]


def backward_call(tick, table, incoming, gain, down, up, loss_grad, limits, saved, state):
    shape = jax.ShapeDtypeStruct
    kept = list(saved) + list(state)
    outs = [shape(item.shape, item.dtype) for item in kept] + [shape((ROWS, WIDTH), BF16)]
    got = pl.pallas_call(
        functools.partial(backward_kernel, tick),
        out_shape=outs,
        in_specs=[SM, VM, VM, VM, VM, ANY, ANY] + [ANY] * 7,
        out_specs=[ANY] * 7 + [VM],
        scratch_shapes=[
            pltpu.VMEM((ROWS, WIDTH), BF16),
            pltpu.VMEM((ROWS, WIDTH // BLOCK), F32),
            pltpu.VMEM((ROWS, WIDTH), BF16),
            pltpu.VMEM((ROWS, NECK), F32),
            pltpu.VMEM((ROWS, 2 * BLOCK), F32),
            pltpu.VMEM((ROWS, WIDTH), BF16),
            pltpu.VMEM((ROWS, NECK), BF16),
            pltpu.VMEM((8, WIDTH), F32),
            pltpu.VMEM((ROWS, WIDTH), F32),
            pltpu.SemaphoreType.DMA((9,)),
        ],
        input_output_aliases={7 + number: number for number in range(7)},
        compiler_params=call_params(24),
        cost_estimate=pl.CostEstimate(flops=150_000_000, bytes_accessed=9_000_000, transcendentals=0),
        name="section_backward",
    )(table, incoming, gain, down, up, loss_grad, limits, *kept)
    return got[:3], got[3:7], got[7]


def empty_buffers(shapes):
    return pl.pallas_call(
        lambda *refs: None,
        out_shape=[jax.ShapeDtypeStruct(dims, kind) for dims, kind in shapes],
        out_specs=[ANY] * len(shapes),
        name="empty_buffers",
    )()


def assemble_kernel(place, *refs):
    parts, outs, sems = refs[:16], refs[16:19], refs[19]
    copies = []
    for number, part in enumerate(parts):
        shard = place[number]
        for which, (start, size) in enumerate(((0, SHARD), (SHARD, SHARD), (2 * SHARD, EXTRA))):
            target = outs[which].at[pl.ds(pl.multiple_of(shard * size, 16), size), :]
            copies.append(
                pltpu.make_async_copy(
                    part.at[pl.ds(start, size), :], target, sems.at[number * 3 + which]
                )
            )
    for copy in copies:
        copy.start()
    for copy in copies:
        copy.wait()


def assemble(place, parts):
    return pl.pallas_call(
        assemble_kernel,
        out_shape=[
            jax.ShapeDtypeStruct((WIDTH, NECK), BF16),
            jax.ShapeDtypeStruct((WIDTH, NECK), BF16),
            jax.ShapeDtypeStruct((16 * EXTRA, NECK), BF16),
        ],
        in_specs=[SM] + [ANY] * 16,
        out_specs=[ANY] * 3,
        scratch_shapes=[pltpu.SemaphoreType.DMA((48,))],
        cost_estimate=pl.CostEstimate(flops=0, bytes_accessed=19_000_000, transcendentals=0),
        name="assemble_weights",
    )(place, *parts)


def fsdp_index(y, z, core):
    return y * 4 + z * 2 + core


def fsdp_pairs(move):
    return [
        (fsdp_index(y, z, core), fsdp_index(*move(y, z, core)))
        for y in range(4)
        for z in range(2)
        for core in range(2)
    ]


def to_core(value):
    return lax.ppermute(value, "fsdp", fsdp_pairs(lambda y, z, core: (y, z, 1 - core)))


def along_z(value):
    return lax.ppermute(value, "fsdp", fsdp_pairs(lambda y, z, core: (y, 1 - z, core)))


def along_y(value, by):
    return lax.ppermute(value, "fsdp", fsdp_pairs(lambda y, z, core: ((y + by) % 4, z, core)))


def gather_parts(own):
    parts = {(0, 0): own}
    parts[(0, 1)] = along_z(own)
    for by in (1, 3, 2):
        parts[(by, 0)] = along_y(own, -by)
    parts[(2, 1)] = along_z(parts[(2, 0)])
    for by in (1, 3):
        parts[(by, 1)] = along_y(parts[(0, 1)], -by)
    return parts


def gradient_kernel(order, normed, neckcot, cot, act, gains, mine, theirs, hold):
    factor = 1.0 / math.sqrt(MICRO * TOKENS * 16)
    core = order[8]
    both = 2 * SHARD
    for number, (left, right) in enumerate(((normed, neckcot), (cot, act))):
        hold[...] = (
            lax.dot_general(left[...], right[...], TN, preferred_element_type=F32) * factor
        ).astype(BF16)
        rows = slice(number * SHARD, (number + 1) * SHARD)
        mine[0, rows, :] = hold[pl.ds(pl.multiple_of(core * SHARD, SHARD), SHARD), :]
        theirs[0, rows, :] = hold[pl.ds(pl.multiple_of((1 - core) * SHARD, SHARD), SHARD), :]
    mine[0, both:, :] = gains[0, core]
    theirs[0, both:, :] = gains[0, 1 - core]


def gradient_blocks(order, first, count, normed, neckcot, cot, act, gains):
    rows = MICRO * TOKENS
    block = pl.BlockSpec((rows, 2 * SHARD), lambda i, order: (0, order[first + i]))
    small = pl.BlockSpec((rows, NECK), lambda i, order: (0, 0))
    result = pl.BlockSpec((1, 2 * SHARD + EXTRA, NECK), lambda i, order: (i, 0, 0))
    return pl.pallas_call(
        gradient_kernel,
        grid_spec=pltpu.PrefetchScalarGridSpec(
            num_scalar_prefetch=1,
            grid=(count,),
            in_specs=[
                block,
                small,
                block,
                small,
                pl.BlockSpec((1, 2, EXTRA, NECK), lambda i, order: (order[first + i], 0, 0, 0)),
            ],
            out_specs=[result, result],
            scratch_shapes=[pltpu.VMEM((2 * SHARD, NECK), BF16)],
        ),
        out_shape=[jax.ShapeDtypeStruct((count, 2 * SHARD + EXTRA, NECK), BF16)] * 2,
        compiler_params=call_params(24),
        name="gradient_blocks",
    )(order, normed, neckcot, cot, act, gains)


REDUCE_ORDER = ((1, 1), (3, 1), (2, 1), (1, 0), (3, 0), (2, 0), (0, 1), (0, 0))


def widen(value):
    return value.astype(F32)


def reduce_parts(order, normed, neckcot, cot, act, gains):
    blocks = {}
    for first in (0, 4):
        mine, theirs = gradient_blocks(order, first, 4, normed, neckcot, cot, act, gains)
        theirs = to_core(theirs)
        for number in range(4):
            blocks[REDUCE_ORDER[first + number]] = (mine[number], theirs[number])

    def summed(key, *others):
        mine, theirs = blocks[key]
        total = widen(mine) + widen(theirs)
        for other in others:
            total += widen(other)
        return total

    def narrow(value):
        return value.astype(BF16)

    first = along_y(narrow(summed((1, 1))), 1)
    second = along_y(narrow(summed((3, 1))), 3)
    third = along_z(narrow(summed((2, 1))))
    fourth = along_y(narrow(summed((1, 0))), 1)
    fifth = along_y(narrow(summed((3, 0))), 3)
    sixth = along_y(narrow(summed((2, 0), third)), 2)
    seventh = along_z(narrow(summed((0, 1), first, second)))
    return summed((0, 0), fourth, fifth, sixth, seventh)


def shards(
    in_base,
    out_base,
    sample_ids,
    send_exponent,
    grad_exponent,
    loss_grad,
    down_weight,
    up_weight,
    norm_gain,
):
    section = lax.axis_index("section")
    place = lax.axis_index("fsdp")
    y, z, core = place >> 2, (place >> 1) & 1, place & 1
    tokens = MICRO * TOKENS
    ticks = CHUNKS + 2 * SECTIONS - 2

    gain_rows = jnp.pad(norm_gain[0], (0, EXTRA * NECK - SHARD)).reshape(EXTRA, NECK)
    own = jnp.concatenate([down_weight[0], up_weight[0], gain_rows], axis=0)
    parts = gather_parts(own)
    pieces, places = [], []
    for (dy, dz), part in parts.items():
        spot = fsdp_index((y + dy) & 3, z ^ dz, core)
        pieces += [part, to_core(part)]
        places += [spot, spot + 1 - 2 * core]
    down, up, gain = assemble(jnp.stack(places).astype(jnp.int32), pieces)
    gain = gain.reshape(16, EXTRA * NECK)[:, :SHARD].reshape(1, WIDTH).astype(F32)

    tick = jnp.arange(ticks, dtype=jnp.int32)

    def lane(chunk):
        active = (chunk >= 0) & (chunk < CHUNKS)
        chunk = jnp.clip(chunk, 0, CHUNKS - 1)
        return active.astype(jnp.int32), chunk

    per = TOKENS // ROWS
    ahead, chunk = lane(tick - section)
    base = sample_ids[chunk // per] * TOKENS + (chunk % per) * ROWS
    back, reverse = lane(tick - 2 * (SECTIONS - 1) + section)
    last = jnp.full((ticks,), section == SECTIONS - 1).astype(jnp.int32)
    table = jnp.stack([ahead, chunk * ROWS, base, back, reverse * ROWS, last], axis=1)

    def limit(exponent):
        exponent = exponent[0].reshape(tokens, WIDTH // BLOCK)
        level = jnp.zeros(exponent.shape, F32)
        for value in range(LOWEST_EXPONENT, HIGHEST_EXPONENT):
            level = jnp.where(exponent == value, F32(CLIP_LEVEL * 2.0**value), level)
        return level

    send_limit, back_limit = limit(send_exponent), limit(grad_exponent)
    base_in = in_base.reshape(-1, WIDTH)
    base_out = out_base.reshape(-1, WIDTH)
    loss = loss_grad.reshape(tokens, WIDTH)

    buffers = empty_buffers(
        [
            ((tokens, WIDTH), BF16),
            ((tokens, WIDTH), BF16),
            ((tokens, NECK), F32),
            ((tokens, NECK), BF16),
            ((tokens, WIDTH), BF16),
            ((tokens, 2 * BLOCK), F32),
            ((tokens, WIDTH), BF16),
            ((tokens, WIDTH), BF16),
            ((tokens, NECK), BF16),
            ((tokens // 2, WIDTH), F32),
        ]
    )
    layer, out, neck, act, normed, stat = buffers[:6]
    cots = buffers[6:]
    zero = jnp.zeros((ROWS, WIDTH), BF16)
    arriving, returning = zero, zero
    for step in range(ticks):
        if step < CHUNKS + SECTIONS - 1:
            (layer, out, neck, act, normed, stat), delivered = forward_call(
                step,
                table,
                arriving,
                gain,
                down,
                up,
                base_in,
                base_out,
                send_limit,
                (layer, out, neck, act, normed, stat),
            )
            pairs = [(s, s + 1) for s in range(SECTIONS - 1) if 0 <= step - s < CHUNKS]
            arriving = lax.ppermute(delivered, "section", pairs) if pairs else zero
        if step >= SECTIONS - 1:
            (layer, neck, stat), cots, sent = backward_call(
                step,
                table,
                returning,
                gain,
                down,
                up,
                loss,
                back_limit,
                (layer, neck, stat),
                cots,
            )
            pairs = [
                (s, s - 1)
                for s in range(1, SECTIONS)
                if 0 <= step - 2 * (SECTIONS - 1) + s < CHUNKS
            ]
            returning = lax.ppermute(sent, "section", pairs) if pairs else zero

    grad, cot, neckcot, gain_sums = cots
    factor = 1.0 / math.sqrt(tokens * 16)
    gains = (jnp.sum(gain_sums, axis=0) * factor).astype(BF16).reshape(8, 2, SHARD)
    gains = jnp.pad(gains, ((0, 0), (0, 0), (0, EXTRA * NECK - SHARD))).reshape(8, 2, EXTRA, NECK)
    order = [((y + dy) & 3) * 2 + (z ^ dz) for dy, dz in REDUCE_ORDER] + [core]
    order = jnp.stack(order).astype(jnp.int32)
    total = reduce_parts(order, normed, neckcot, cot, act, gains)
    shape = (1, MICRO, TOKENS, WIDTH)
    return (
        out.reshape(shape),
        grad.reshape(shape),
        total[None, :SHARD],
        total[None, SHARD : 2 * SHARD],
        total[2 * SHARD :].reshape(1, EXTRA * NECK)[:, :SHARD],
    )


def solution(mesh):
    in_specs = (
        P("section", None, "fsdp", None),
        P("section", None, "fsdp", None),
        P(),
        P("section", None, "fsdp", None),
        P("section", None, "fsdp", None),
        P(None, "fsdp", None),
        P("section", "fsdp", None),
        P("section", "fsdp", None),
        P("section", "fsdp"),
    )
    out_specs = (
        P("section", None, "fsdp", None),
        P("section", None, "fsdp", None),
        P("section", "fsdp", None),
        P("section", "fsdp", None),
        P("section", "fsdp"),
    )
    return jax.shard_map(shards, mesh=mesh, in_specs=in_specs, out_specs=out_specs, check_vma=False)
```

```python
import functools
import math

import jax
import jax.numpy as jnp
from jax import lax
from jax.experimental import pallas as pl
from jax.experimental.pallas import tpu as pltpu
from jax.sharding import PartitionSpec as P

SQRT_HALF = 0.7071067811865476
INV_ROOT_TAU = 0.3989422804014327
CLIP_LEVEL = 448.0
NORM_EPSILON = 1e-05
LOWEST_EXPONENT = -9
HIGHEST_EXPONENT = -3

SECTIONS = 8
WIDTH = 9216
NECK = 256
BLOCK = 128
TOKENS = 48
MICRO = 4
ROWS = 16
CHUNKS = MICRO * TOKENS // ROWS
SHARD = 576
EXTRA = 16
WIDE = 1024
MEDIUM = 512

VM = pl.BlockSpec(memory_space=pltpu.VMEM)
SM = pl.BlockSpec(memory_space=pltpu.SMEM)
ANY = pl.BlockSpec(memory_space=pltpu.HBM)
NT = (((1,), (1,)), ((), ()))
TN = (((0,), (0,)), ((), ()))
F32 = jnp.float32
BF16 = jnp.bfloat16


def in_hbm(value):
    return pltpu.with_memory_space_constraint(value, pltpu.HBM)


def lane_sum(values):
    return jnp.sum(values, axis=-1, keepdims=True)


def gain_row(gain, start, size):
    first = start // BLOCK
    rows = [gain[first + number : first + number + 1, :] for number in range(size // BLOCK)]
    return jnp.concatenate(rows, axis=1)


def clipped(values, limits, start):
    pieces = []
    for offset in range(0, values.shape[1], BLOCK):
        index = (start + offset) // BLOCK
        bound = jnp.broadcast_to(limits[:, index : index + 1], (values.shape[0], BLOCK))
        pieces.append(jnp.clip(values[:, offset : offset + BLOCK], -bound, bound))
    return jnp.concatenate(pieces, axis=1).astype(BF16)


def forward_kernel(
    tick,
    table,
    incoming,
    gain,
    down,
    up,
    base_in,
    base_out,
    limits,
    *refs,
):
    (outs, scratch) = (refs[6:13], refs[13:])
    layer_all, out_all, neck_all, act_all, normed_all, stat_all, delivered = outs
    rows_in, rows_out, bound, layer, section, neck, act, normed, stat, sems = scratch

    @pl.when(table[tick, 0] == 1)
    def _():
        row = pl.multiple_of(table[tick, 1], ROWS)
        base = pl.multiple_of(table[tick, 2], ROWS)
        here = pl.ds(row, ROWS)
        loads = [
            pltpu.make_async_copy(base_in.at[pl.ds(base, ROWS), :], rows_in, sems.at[0]),
            pltpu.make_async_copy(base_out.at[pl.ds(base, ROWS), :], rows_out, sems.at[1]),
            pltpu.make_async_copy(limits.at[here, :], bound, sems.at[2]),
        ]
        for copy in loads:
            copy.start()
        stores = [
            pltpu.make_async_copy(source, target.at[here, :], sems.at[3 + number])
            for number, (source, target) in enumerate(
                (
                    (layer, layer_all),
                    (section, out_all),
                    (neck, neck_all),
                    (act, act_all),
                    (normed, normed_all),
                    (stat, stat_all),
                )
            )
        ]
        loads[0].wait()
        total = jnp.zeros((ROWS, BLOCK), F32)
        for start in range(0, WIDTH, WIDE):
            span = slice(start, start + WIDE)
            values = (rows_in[:, span].astype(F32) + incoming[:, span].astype(F32)).astype(BF16)
            layer[:, span] = values
            values = values.astype(F32)
            for offset in range(0, WIDE, BLOCK):
                total += values[:, offset : offset + BLOCK]
        stores[0].start()
        mean = lane_sum(total) * (1.0 / WIDTH)
        total = jnp.zeros((ROWS, BLOCK), F32)
        for start in range(0, WIDTH, WIDE):
            values = layer[:, start : start + WIDE].astype(F32) - mean
            values = values * values
            for offset in range(0, WIDE, BLOCK):
                total += values[:, offset : offset + BLOCK]
        scale = lax.rsqrt(lane_sum(total) * (1.0 / WIDTH) + NORM_EPSILON)
        stat[:, :BLOCK] = jnp.broadcast_to(mean, (ROWS, BLOCK))
        stat[:, BLOCK:] = jnp.broadcast_to(scale, (ROWS, BLOCK))
        stores[5].start()
        result = jnp.zeros((ROWS, NECK), F32)
        for start in range(0, WIDTH, WIDE):
            span = slice(start, start + WIDE)
            values = (layer[:, span].astype(F32) - mean) * scale
            values = (values * gain_row(gain, start, WIDE)).astype(BF16)
            normed[:, span] = values
            result += jnp.dot(values, down[span, :], preferred_element_type=F32)
        stores[4].start()
        neck[...] = result
        stores[2].start()
        activated = (result * 0.5 * (1.0 + lax.erf(result * SQRT_HALF))).astype(BF16)
        act[...] = activated
        stores[3].start()
        loads[1].wait()
        loads[2].wait()
        edges = bound[...]
        for start in range(0, WIDTH, MEDIUM):
            span = slice(start, start + MEDIUM)
            branch = lax.dot_general(activated, up[span, :], NT, preferred_element_type=F32)
            value = (layer[:, span].astype(F32) + branch).astype(BF16)
            section[:, span] = value
            change = value.astype(F32) - rows_out[:, span].astype(F32)
            delivered[:, span] = clipped(change, edges, start)
        stores[1].start()
        for copy in stores:
            copy.wait()


def backward_kernel(
    tick,
    table,
    incoming,
    gain,
    down,
    up,
    loss_grad,
    limits,
    layer_all,
    neck_all,
    stat_all,
    *refs,
):
    (outs, scratch) = (refs[4:12], refs[12:])
    gain_before = refs[3]
    grad_all, cot_all, neckcot_all, gain_sums, sent = outs[3:]
    cot, bound, layer, neck, stat, grad, neckcot, hold, sems = scratch

    gain_sums[...] = gain_before[...]

    @pl.when(table[tick, 3] == 1)
    def _():
        row = pl.multiple_of(table[tick, 4], ROWS)
        here = pl.ds(row, ROWS)
        last = table[tick, 5] == 1
        loads = [
            pltpu.make_async_copy(limits.at[here, :], bound, sems.at[0]),
            pltpu.make_async_copy(layer_all.at[here, :], layer, sems.at[1]),
            pltpu.make_async_copy(neck_all.at[here, :], neck, sems.at[2]),
            pltpu.make_async_copy(stat_all.at[here, :], stat, sems.at[3]),
        ]
        for copy in loads:
            copy.start()
        stores = [
            pltpu.make_async_copy(grad, grad_all.at[here, :], sems.at[4]),
            pltpu.make_async_copy(cot, cot_all.at[here, :], sems.at[5]),
            pltpu.make_async_copy(neckcot, neckcot_all.at[here, :], sems.at[6]),
        ]

        @pl.when(last)
        def _():
            fetch = pltpu.make_async_copy(loss_grad.at[here, :], cot, sems.at[8])
            fetch.start()
            fetch.wait()

        @pl.when(jnp.logical_not(last))
        def _():
            cot[...] = incoming[...]

        stores[1].start()
        result = jnp.zeros((ROWS, NECK), F32)
        for start in range(0, WIDTH, WIDE):
            span = slice(start, start + WIDE)
            result += jnp.dot(cot[:, span], up[span, :], preferred_element_type=F32)
        loads[2].wait()
        bottle = neck[...]
        slope = 0.5 * (1.0 + lax.erf(bottle * SQRT_HALF)) + bottle * INV_ROOT_TAU * jnp.exp(
            -0.5 * bottle * bottle
        )
        small = (result * slope).astype(BF16)
        neckcot[...] = small
        stores[2].start()
        loads[1].wait()
        loads[3].wait()
        mean = stat[:, :1]
        scale = stat[:, BLOCK : BLOCK + 1]
        first = jnp.zeros((ROWS, BLOCK), F32)
        second = jnp.zeros((ROWS, BLOCK), F32)
        for start in range(0, WIDTH, MEDIUM):
            span = slice(start, start + MEDIUM)
            wide = lax.dot_general(small, down[span, :], NT, preferred_element_type=F32)
            centred = (layer[:, span].astype(F32) - mean) * scale
            product = wide * centred
            gain_sums[:, span] += product[:8, :] + product[8:, :]
            scaled = wide * gain_row(gain, start, MEDIUM)
            hold[:, span] = scaled
            product = scaled * centred
            for offset in range(0, MEDIUM, BLOCK):
                first += scaled[:, offset : offset + BLOCK]
                second += product[:, offset : offset + BLOCK]
        first = lane_sum(first) * (1.0 / WIDTH)
        second = lane_sum(second) * (1.0 / WIDTH)
        loads[0].wait()
        edges = bound[...]
        for start in range(0, WIDTH, MEDIUM):
            span = slice(start, start + MEDIUM)
            centred = (layer[:, span].astype(F32) - mean) * scale
            value = cot[:, span].astype(F32) + scale * (hold[:, span] - first - centred * second)
            grad[:, span] = value.astype(BF16)
            sent[:, span] = clipped(value, edges, start)
        stores[0].start()
        for copy in stores:
            copy.wait()


def call_params(megabytes):
    return pltpu.CompilerParams(vmem_limit_bytes=megabytes << 20)


def forward_call(tick, table, incoming, gain, down, up, base_in, base_out, limits, state):
    shape = jax.ShapeDtypeStruct
    outs = [shape(item.shape, item.dtype) for item in state] + [shape((ROWS, WIDTH), BF16)]
    got = pl.pallas_call(
        functools.partial(forward_kernel, tick),
        out_shape=outs,
        in_specs=[SM, VM, VM, VM, VM, ANY, ANY, ANY] + [ANY] * 6,
        out_specs=[ANY] * 6 + [VM],
        scratch_shapes=[
            pltpu.VMEM((ROWS, WIDTH), BF16),
            pltpu.VMEM((ROWS, WIDTH), BF16),
            pltpu.VMEM((ROWS, WIDTH // BLOCK), F32),
            pltpu.VMEM((ROWS, WIDTH), BF16),
            pltpu.VMEM((ROWS, WIDTH), BF16),
            pltpu.VMEM((ROWS, NECK), F32),
            pltpu.VMEM((ROWS, NECK), BF16),
            pltpu.VMEM((ROWS, WIDTH), BF16),
            pltpu.VMEM((ROWS, 2 * BLOCK), F32),
            pltpu.SemaphoreType.DMA((9,)),
        ],
        input_output_aliases={8 + number: number for number in range(6)},
        compiler_params=call_params(8),
        cost_estimate=pl.CostEstimate(flops=150_000_000, bytes_accessed=9_000_000, transcendentals=0),
        name="section_forward",
    )(table, incoming, gain, down, up, in_hbm(base_in), in_hbm(base_out), limits, *map(in_hbm, state))
    return got[:6], got[6]


def backward_call(tick, table, incoming, gain, down, up, loss_grad, limits, saved, state):
    shape = jax.ShapeDtypeStruct
    kept = list(saved) + list(state)
    outs = [shape(item.shape, item.dtype) for item in kept] + [shape((ROWS, WIDTH), BF16)]
    got = pl.pallas_call(
        functools.partial(backward_kernel, tick),
        out_shape=outs,
        in_specs=[SM, VM, VM, VM, VM, ANY, ANY] + [ANY] * 6 + [VM],
        out_specs=[ANY] * 6 + [VM, VM],
        scratch_shapes=[
            pltpu.VMEM((ROWS, WIDTH), BF16),
            pltpu.VMEM((ROWS, WIDTH // BLOCK), F32),
            pltpu.VMEM((ROWS, WIDTH), BF16),
            pltpu.VMEM((ROWS, NECK), F32),
            pltpu.VMEM((ROWS, 2 * BLOCK), F32),
            pltpu.VMEM((ROWS, WIDTH), BF16),
            pltpu.VMEM((ROWS, NECK), BF16),
            pltpu.VMEM((ROWS, WIDTH), F32),
            pltpu.SemaphoreType.DMA((9,)),
        ],
        input_output_aliases={7 + number: number for number in range(7)},
        compiler_params=call_params(8),
        cost_estimate=pl.CostEstimate(flops=150_000_000, bytes_accessed=9_000_000, transcendentals=0),
        name="section_backward",
    )(table, incoming, gain, down, up, in_hbm(loss_grad), limits, *map(in_hbm, kept[:-1]), kept[-1])
    return got[:3], got[3:7], got[7]


def empty_buffers(shapes):
    return pl.pallas_call(
        lambda *refs: None,
        out_shape=[jax.ShapeDtypeStruct(dims, kind) for dims, kind in shapes],
        out_specs=[ANY] * len(shapes),
        name="empty_buffers",
    )()


def assemble_kernel(place, *refs):
    parts, (down, up, gain) = refs[:16], refs[16:]
    per = 2 * SHARD // BLOCK
    for number, part in enumerate(parts):
        shard = place[number]
        rows = pl.ds(pl.multiple_of(shard * SHARD, SHARD), SHARD)
        down[rows, :] = part[:SHARD, :]
        up[rows, :] = part[SHARD : 2 * SHARD, :]
        if number % 2 == 0:
            piece = part[2 * SHARD :, :BLOCK].astype(F32)
            for line in range(per):
                gain[pl.ds((shard >> 1) * per + line, 1), :] = piece[line : line + 1, :]


def assemble(place, parts):
    return pl.pallas_call(
        assemble_kernel,
        out_shape=[
            jax.ShapeDtypeStruct((WIDTH, NECK), BF16),
            jax.ShapeDtypeStruct((WIDTH, NECK), BF16),
            jax.ShapeDtypeStruct((WIDTH // BLOCK, BLOCK), F32),
        ],
        in_specs=[SM] + [VM] * 16,
        out_specs=[VM] * 3,
        compiler_params=call_params(8),
        cost_estimate=pl.CostEstimate(flops=0, bytes_accessed=19_000_000, transcendentals=0),
        name="assemble_weights",
    )(place, *parts)


def fsdp_index(y, z, core):
    return y * 4 + z * 2 + core


def fsdp_pairs(move):
    return [
        (fsdp_index(y, z, core), fsdp_index(*move(y, z, core)))
        for y in range(4)
        for z in range(2)
        for core in range(2)
    ]


def to_core(value):
    return lax.ppermute(value, "fsdp", fsdp_pairs(lambda y, z, core: (y, z, 1 - core)))


def along_z(value):
    return lax.ppermute(value, "fsdp", fsdp_pairs(lambda y, z, core: (y, 1 - z, core)))


def along_y(value, by):
    return lax.ppermute(value, "fsdp", fsdp_pairs(lambda y, z, core: ((y + by) % 4, z, core)))


def gather_parts(own):
    parts = {(0, 0): own}
    parts[(0, 1)] = along_z(own)
    for by in (1, 3, 2):
        parts[(by, 0)] = along_y(own, -by)
    parts[(2, 1)] = along_z(parts[(2, 0)])
    for by in (1, 3):
        parts[(by, 1)] = along_y(parts[(0, 1)], -by)
    return parts


def gradient_kernel(order, normed, neckcot, cot, act, gains, mine, theirs, hold):
    factor = 1.0 / math.sqrt(MICRO * TOKENS * 16)
    core = order[8]
    both = 2 * SHARD
    for number, (left, right) in enumerate(((normed, neckcot), (cot, act))):
        hold[...] = (
            lax.dot_general(left[...], right[...], TN, preferred_element_type=F32) * factor
        ).astype(BF16)
        rows = slice(number * SHARD, (number + 1) * SHARD)
        mine[0, rows, :] = hold[pl.ds(pl.multiple_of(core * SHARD, SHARD), SHARD), :]
        theirs[0, rows, :] = hold[pl.ds(pl.multiple_of((1 - core) * SHARD, SHARD), SHARD), :]
    sums = jnp.sum(gains[...], axis=0, keepdims=True) * factor
    lines = [sums[:, start : start + BLOCK] for start in range(0, both, BLOCK)]
    lines.append(jnp.zeros((EXTRA - len(lines), BLOCK), F32))
    lines = jnp.concatenate(lines, axis=0).astype(BF16)
    lines = jnp.concatenate([lines, lines], axis=1)
    mine[0, both:, :] = lines
    theirs[0, both:, :] = lines


def gradient_blocks(order, first, count, normed, neckcot, cot, act, gains):
    rows = MICRO * TOKENS
    block = pl.BlockSpec((rows, 2 * SHARD), lambda i, order: (0, order[first + i]))
    small = pl.BlockSpec((rows, NECK), lambda i, order: (0, 0))
    result = pl.BlockSpec((1, 2 * SHARD + EXTRA, NECK), lambda i, order: (i, 0, 0))
    return pl.pallas_call(
        gradient_kernel,
        grid_spec=pltpu.PrefetchScalarGridSpec(
            num_scalar_prefetch=1,
            grid=(count,),
            in_specs=[
                block,
                small,
                block,
                small,
                pl.BlockSpec((8, 2 * SHARD), lambda i, order: (0, order[first + i])),
            ],
            out_specs=[result, result],
            scratch_shapes=[pltpu.VMEM((2 * SHARD, NECK), BF16)],
        ),
        out_shape=[jax.ShapeDtypeStruct((count, 2 * SHARD + EXTRA, NECK), BF16)] * 2,
        compiler_params=call_params(8),
        name="gradient_blocks",
    )(order, in_hbm(normed), neckcot, in_hbm(cot), act, gains)


REDUCE_ORDER = ((1, 1), (3, 1), (2, 1), (1, 0), (3, 0), (2, 0), (0, 1), (0, 0))


def widen(value):
    return value.astype(F32)


def reduce_parts(order, normed, neckcot, cot, act, gains):
    blocks = {}
    for first in (0, 4):
        mine, theirs = gradient_blocks(order, first, 4, normed, neckcot, cot, act, gains)
        theirs = to_core(theirs)
        for number in range(4):
            blocks[REDUCE_ORDER[first + number]] = (mine[number], theirs[number])

    def summed(key, *others):
        mine, theirs = blocks[key]
        total = widen(mine) + widen(theirs)
        for other in others:
            total += widen(other)
        return total

    def narrow(value):
        return value.astype(BF16)

    first = along_y(narrow(summed((1, 1))), 1)
    second = along_y(narrow(summed((3, 1))), 3)
    third = along_z(narrow(summed((2, 1))))
    fourth = along_y(narrow(summed((1, 0))), 1)
    fifth = along_y(narrow(summed((3, 0))), 3)
    sixth = along_y(narrow(summed((2, 0), third)), 2)
    seventh = along_z(narrow(summed((0, 1), first, second)))
    return summed((0, 0), fourth, fifth, sixth, seventh)


def shards(
    in_base,
    out_base,
    sample_ids,
    send_exponent,
    grad_exponent,
    loss_grad,
    down_weight,
    up_weight,
    norm_gain,
):
    section = lax.axis_index("section")
    place = lax.axis_index("fsdp")
    y, z, core = place >> 2, (place >> 1) & 1, place & 1
    tokens = MICRO * TOKENS
    ticks = CHUNKS + 2 * SECTIONS - 2

    other = to_core(norm_gain)
    pair = jnp.where(
        core == 0,
        jnp.concatenate([norm_gain, other], axis=1),
        jnp.concatenate([other, norm_gain], axis=1),
    ).reshape(2 * SHARD // BLOCK, BLOCK)
    gain_rows = jnp.pad(pair, ((0, EXTRA - pair.shape[0]), (0, NECK - BLOCK)))
    own = jnp.concatenate([down_weight[0], up_weight[0], gain_rows], axis=0)
    parts = gather_parts(own)
    pieces, places = [], []
    for (dy, dz), part in parts.items():
        spot = fsdp_index((y + dy) & 3, z ^ dz, core)
        pieces += [part, to_core(part)]
        places += [spot, spot + 1 - 2 * core]
    down, up, gain = assemble(jnp.stack(places).astype(jnp.int32), pieces)

    tick = jnp.arange(ticks, dtype=jnp.int32)

    def lane(chunk):
        active = (chunk >= 0) & (chunk < CHUNKS)
        chunk = jnp.clip(chunk, 0, CHUNKS - 1)
        return active.astype(jnp.int32), chunk

    per = TOKENS // ROWS
    ahead, chunk = lane(tick - section)
    base = sample_ids[chunk // per] * TOKENS + (chunk % per) * ROWS
    back, reverse = lane(tick - 2 * (SECTIONS - 1) + section)
    last = jnp.full((ticks,), section == SECTIONS - 1).astype(jnp.int32)
    table = jnp.stack([ahead, chunk * ROWS, base, back, reverse * ROWS, last], axis=1)

    def limit(exponent):
        exponent = exponent[0].reshape(tokens, WIDTH // BLOCK)
        level = jnp.zeros(exponent.shape, F32)
        for value in range(LOWEST_EXPONENT, HIGHEST_EXPONENT):
            level = jnp.where(exponent == value, F32(CLIP_LEVEL * 2.0**value), level)
        return level

    send_limit, back_limit = limit(send_exponent), limit(grad_exponent)
    base_in = in_base.reshape(-1, WIDTH)
    base_out = out_base.reshape(-1, WIDTH)
    loss = loss_grad.reshape(tokens, WIDTH)

    buffers = empty_buffers(
        [
            ((tokens, WIDTH), BF16),
            ((tokens, WIDTH), BF16),
            ((tokens, NECK), F32),
            ((tokens, NECK), BF16),
            ((tokens, WIDTH), BF16),
            ((tokens, 2 * BLOCK), F32),
            ((tokens, WIDTH), BF16),
            ((tokens, WIDTH), BF16),
            ((tokens, NECK), BF16),
        ]
    )
    layer, out, neck, act, normed, stat = buffers[:6]
    cots = [*buffers[6:], jnp.zeros((8, WIDTH), F32)]
    zero = jnp.zeros((ROWS, WIDTH), BF16)
    arriving, returning = zero, zero
    for step in range(ticks):
        if step < CHUNKS + SECTIONS - 1:
            (layer, out, neck, act, normed, stat), delivered = forward_call(
                step,
                table,
                arriving,
                gain,
                down,
                up,
                base_in,
                base_out,
                send_limit,
                (layer, out, neck, act, normed, stat),
            )
            pairs = [(s, s + 1) for s in range(SECTIONS - 1) if 0 <= step - s < CHUNKS]
            arriving = lax.ppermute(delivered, "section", pairs) if pairs else zero
        if step >= SECTIONS - 1:
            (layer, neck, stat), cots, sent = backward_call(
                step,
                table,
                returning,
                gain,
                down,
                up,
                loss,
                back_limit,
                (layer, neck, stat),
                cots,
            )
            pairs = [
                (s, s - 1)
                for s in range(1, SECTIONS)
                if 0 <= step - 2 * (SECTIONS - 1) + s < CHUNKS
            ]
            returning = lax.ppermute(sent, "section", pairs) if pairs else zero

    grad, cot, neckcot, gain_sums = cots
    order = [((y + dy) & 3) * 2 + (z ^ dz) for dy, dz in REDUCE_ORDER] + [core]
    order = jnp.stack(order).astype(jnp.int32)
    total = reduce_parts(order, normed, neckcot, cot, act, gain_sums)
    shape = (1, MICRO, TOKENS, WIDTH)
    return (
        out.reshape(shape),
        grad.reshape(shape),
        total[None, :SHARD],
        total[None, SHARD : 2 * SHARD],
        lax.dynamic_slice_in_dim(
            total[2 * SHARD : 2 * SHARD + 9, :BLOCK].reshape(1, 2 * SHARD), core * SHARD, SHARD, 1
        ),
    )


def solution(mesh):
    in_specs = (
        P("section", None, "fsdp", None),
        P("section", None, "fsdp", None),
        P(),
        P("section", None, "fsdp", None),
        P("section", None, "fsdp", None),
        P(None, "fsdp", None),
        P("section", "fsdp", None),
        P("section", "fsdp", None),
        P("section", "fsdp"),
    )
    out_specs = (
        P("section", None, "fsdp", None),
        P("section", None, "fsdp", None),
        P("section", "fsdp", None),
        P("section", "fsdp", None),
        P("section", "fsdp"),
    )
    return jax.shard_map(shards, mesh=mesh, in_specs=in_specs, out_specs=out_specs, check_vma=False)
```

```python
import functools
import math

import jax
import jax.numpy as jnp
from jax import lax
from jax.experimental import pallas as pl
from jax.experimental.pallas import tpu as pltpu
from jax.sharding import PartitionSpec as P

SQRT_HALF = 0.7071067811865476
INV_ROOT_TAU = 0.3989422804014327
CLIP_LEVEL = 448.0
NORM_EPSILON = 1e-05
LOWEST_EXPONENT = -9
HIGHEST_EXPONENT = -3

SECTIONS = 8
WIDTH = 9216
NECK = 256
BLOCK = 128
TOKENS = 48
MICRO = 4
ROWS = 16
CHUNKS = MICRO * TOKENS // ROWS
SHARD = 576
STRIDE = 2
DEPTH = STRIDE * (SECTIONS - 1)
EXTRA = 16
WIDE = 1024
MEDIUM = 512

VM = pl.BlockSpec(memory_space=pltpu.VMEM)
SM = pl.BlockSpec(memory_space=pltpu.SMEM)
ANY = pl.BlockSpec(memory_space=pltpu.HBM)
NT = (((1,), (1,)), ((), ()))
TN = (((0,), (0,)), ((), ()))
F32 = jnp.float32
BF16 = jnp.bfloat16


def in_hbm(value):
    return pltpu.with_memory_space_constraint(value, pltpu.HBM)


def lane_sum(values):
    return jnp.sum(values, axis=-1, keepdims=True)


def gain_row(gain, start, size):
    first = start // BLOCK
    rows = [gain[first + number : first + number + 1, :] for number in range(size // BLOCK)]
    return jnp.concatenate(rows, axis=1)


def clipped(values, limits, start):
    pieces = []
    for offset in range(0, values.shape[1], BLOCK):
        index = (start + offset) // BLOCK
        bound = jnp.broadcast_to(limits[:, index : index + 1], (values.shape[0], BLOCK))
        pieces.append(jnp.clip(values[:, offset : offset + BLOCK], -bound, bound))
    return jnp.concatenate(pieces, axis=1).astype(BF16)


def forward_kernel(
    tick,
    table,
    incoming,
    gain,
    down,
    up,
    base_in,
    base_out,
    limits,
    *refs,
):
    (outs, scratch) = (refs[6:13], refs[13:])
    layer_all, out_all, neck_all, act_all, normed_all, stat_all, delivered = outs
    rows_in, rows_out, bound, layer, section, neck, act, normed, stat, sems = scratch

    @pl.when(table[tick, 0] == 1)
    def _():
        row = pl.multiple_of(table[tick, 1], ROWS)
        base = pl.multiple_of(table[tick, 2], ROWS)
        here = pl.ds(row, ROWS)
        loads = [
            pltpu.make_async_copy(base_in.at[pl.ds(base, ROWS), :], rows_in, sems.at[0]),
            pltpu.make_async_copy(base_out.at[pl.ds(base, ROWS), :], rows_out, sems.at[1]),
            pltpu.make_async_copy(limits.at[here, :], bound, sems.at[2]),
        ]
        for copy in loads:
            copy.start()
        stores = [
            pltpu.make_async_copy(source, target.at[here, :], sems.at[3 + number])
            for number, (source, target) in enumerate(
                (
                    (layer, layer_all),
                    (section, out_all),
                    (neck, neck_all),
                    (act, act_all),
                    (normed, normed_all),
                    (stat, stat_all),
                )
            )
        ]
        loads[0].wait()
        total = jnp.zeros((ROWS, BLOCK), F32)
        for start in range(0, WIDTH, WIDE):
            span = slice(start, start + WIDE)
            values = (rows_in[:, span].astype(F32) + incoming[:, span].astype(F32)).astype(BF16)
            layer[:, span] = values
            values = values.astype(F32)
            for offset in range(0, WIDE, BLOCK):
                total += values[:, offset : offset + BLOCK]
        stores[0].start()
        mean = lane_sum(total) * (1.0 / WIDTH)
        total = jnp.zeros((ROWS, BLOCK), F32)
        for start in range(0, WIDTH, WIDE):
            values = layer[:, start : start + WIDE].astype(F32) - mean
            values = values * values
            for offset in range(0, WIDE, BLOCK):
                total += values[:, offset : offset + BLOCK]
        scale = lax.rsqrt(lane_sum(total) * (1.0 / WIDTH) + NORM_EPSILON)
        stat[:, :BLOCK] = jnp.broadcast_to(mean, (ROWS, BLOCK))
        stat[:, BLOCK:] = jnp.broadcast_to(scale, (ROWS, BLOCK))
        stores[5].start()
        result = jnp.zeros((ROWS, NECK), F32)
        for start in range(0, WIDTH, WIDE):
            span = slice(start, start + WIDE)
            values = (layer[:, span].astype(F32) - mean) * scale
            values = (values * gain_row(gain, start, WIDE)).astype(BF16)
            normed[:, span] = values
            result += jnp.dot(values, down[span, :], preferred_element_type=F32)
        stores[4].start()
        neck[...] = result
        stores[2].start()
        activated = (result * 0.5 * (1.0 + lax.erf(result * SQRT_HALF))).astype(BF16)
        act[...] = activated
        stores[3].start()
        loads[1].wait()
        loads[2].wait()
        edges = bound[...]
        for start in range(0, WIDTH, MEDIUM):
            span = slice(start, start + MEDIUM)
            branch = lax.dot_general(activated, up[span, :], NT, preferred_element_type=F32)
            value = (layer[:, span].astype(F32) + branch).astype(BF16)
            section[:, span] = value
            change = value.astype(F32) - rows_out[:, span].astype(F32)
            delivered[:, span] = clipped(change, edges, start)
        stores[1].start()
        for copy in stores:
            copy.wait()


def backward_kernel(
    tick,
    table,
    incoming,
    gain,
    down,
    up,
    loss_grad,
    limits,
    layer_all,
    neck_all,
    stat_all,
    *refs,
):
    (outs, scratch) = (refs[4:12], refs[12:])
    gain_before = refs[3]
    grad_all, cot_all, neckcot_all, gain_sums, sent = outs[3:]
    cot, bound, layer, neck, stat, grad, neckcot, hold, sems = scratch

    gain_sums[...] = gain_before[...]

    @pl.when(table[tick, 3] == 1)
    def _():
        row = pl.multiple_of(table[tick, 4], ROWS)
        here = pl.ds(row, ROWS)
        last = table[tick, 5] == 1
        loads = [
            pltpu.make_async_copy(limits.at[here, :], bound, sems.at[0]),
            pltpu.make_async_copy(layer_all.at[here, :], layer, sems.at[1]),
            pltpu.make_async_copy(neck_all.at[here, :], neck, sems.at[2]),
            pltpu.make_async_copy(stat_all.at[here, :], stat, sems.at[3]),
        ]
        for copy in loads:
            copy.start()
        stores = [
            pltpu.make_async_copy(grad, grad_all.at[here, :], sems.at[4]),
            pltpu.make_async_copy(cot, cot_all.at[here, :], sems.at[5]),
            pltpu.make_async_copy(neckcot, neckcot_all.at[here, :], sems.at[6]),
        ]

        @pl.when(last)
        def _():
            fetch = pltpu.make_async_copy(loss_grad.at[here, :], cot, sems.at[8])
            fetch.start()
            fetch.wait()

        @pl.when(jnp.logical_not(last))
        def _():
            cot[...] = incoming[...]

        stores[1].start()
        result = jnp.zeros((ROWS, NECK), F32)
        for start in range(0, WIDTH, WIDE):
            span = slice(start, start + WIDE)
            result += jnp.dot(cot[:, span], up[span, :], preferred_element_type=F32)
        loads[2].wait()
        bottle = neck[...]
        slope = 0.5 * (1.0 + lax.erf(bottle * SQRT_HALF)) + bottle * INV_ROOT_TAU * jnp.exp(
            -0.5 * bottle * bottle
        )
        small = (result * slope).astype(BF16)
        neckcot[...] = small
        stores[2].start()
        loads[1].wait()
        loads[3].wait()
        mean = stat[:, :1]
        scale = stat[:, BLOCK : BLOCK + 1]
        first = jnp.zeros((ROWS, BLOCK), F32)
        second = jnp.zeros((ROWS, BLOCK), F32)
        for start in range(0, WIDTH, MEDIUM):
            span = slice(start, start + MEDIUM)
            wide = lax.dot_general(small, down[span, :], NT, preferred_element_type=F32)
            centred = (layer[:, span].astype(F32) - mean) * scale
            product = wide * centred
            gain_sums[:, span] += product[:8, :] + product[8:, :]
            scaled = wide * gain_row(gain, start, MEDIUM)
            hold[:, span] = scaled
            product = scaled * centred
            for offset in range(0, MEDIUM, BLOCK):
                first += scaled[:, offset : offset + BLOCK]
                second += product[:, offset : offset + BLOCK]
        first = lane_sum(first) * (1.0 / WIDTH)
        second = lane_sum(second) * (1.0 / WIDTH)
        loads[0].wait()
        edges = bound[...]
        for start in range(0, WIDTH, MEDIUM):
            span = slice(start, start + MEDIUM)
            centred = (layer[:, span].astype(F32) - mean) * scale
            value = cot[:, span].astype(F32) + scale * (hold[:, span] - first - centred * second)
            grad[:, span] = value.astype(BF16)
            sent[:, span] = clipped(value, edges, start)
        stores[0].start()
        for copy in stores:
            copy.wait()


def call_params(megabytes):
    return pltpu.CompilerParams(vmem_limit_bytes=megabytes << 20)


def forward_call(tick, table, incoming, gain, down, up, base_in, base_out, limits, state):
    shape = jax.ShapeDtypeStruct
    outs = [shape(item.shape, item.dtype) for item in state] + [shape((ROWS, WIDTH), BF16)]
    got = pl.pallas_call(
        functools.partial(forward_kernel, tick),
        out_shape=outs,
        in_specs=[SM, VM, VM, VM, VM, ANY, ANY, ANY] + [ANY] * 6,
        out_specs=[ANY] * 6 + [VM],
        scratch_shapes=[
            pltpu.VMEM((ROWS, WIDTH), BF16),
            pltpu.VMEM((ROWS, WIDTH), BF16),
            pltpu.VMEM((ROWS, WIDTH // BLOCK), F32),
            pltpu.VMEM((ROWS, WIDTH), BF16),
            pltpu.VMEM((ROWS, WIDTH), BF16),
            pltpu.VMEM((ROWS, NECK), F32),
            pltpu.VMEM((ROWS, NECK), BF16),
            pltpu.VMEM((ROWS, WIDTH), BF16),
            pltpu.VMEM((ROWS, 2 * BLOCK), F32),
            pltpu.SemaphoreType.DMA((9,)),
        ],
        input_output_aliases={8 + number: number for number in range(6)},
        compiler_params=call_params(8),
        cost_estimate=pl.CostEstimate(flops=150_000_000, bytes_accessed=9_000_000, transcendentals=0),
        name="section_forward",
    )(table, incoming, gain, down, up, in_hbm(base_in), in_hbm(base_out), limits, *map(in_hbm, state))
    return got[:6], got[6]


def backward_call(tick, table, incoming, gain, down, up, loss_grad, limits, saved, state):
    shape = jax.ShapeDtypeStruct
    kept = list(saved) + list(state)
    outs = [shape(item.shape, item.dtype) for item in kept] + [shape((ROWS, WIDTH), BF16)]
    got = pl.pallas_call(
        functools.partial(backward_kernel, tick),
        out_shape=outs,
        in_specs=[SM, VM, VM, VM, VM, ANY, ANY] + [ANY] * 6 + [VM],
        out_specs=[ANY] * 6 + [VM, VM],
        scratch_shapes=[
            pltpu.VMEM((ROWS, WIDTH), BF16),
            pltpu.VMEM((ROWS, WIDTH // BLOCK), F32),
            pltpu.VMEM((ROWS, WIDTH), BF16),
            pltpu.VMEM((ROWS, NECK), F32),
            pltpu.VMEM((ROWS, 2 * BLOCK), F32),
            pltpu.VMEM((ROWS, WIDTH), BF16),
            pltpu.VMEM((ROWS, NECK), BF16),
            pltpu.VMEM((ROWS, WIDTH), F32),
            pltpu.SemaphoreType.DMA((9,)),
        ],
        input_output_aliases={7 + number: number for number in range(7)},
        compiler_params=call_params(8),
        cost_estimate=pl.CostEstimate(flops=150_000_000, bytes_accessed=9_000_000, transcendentals=0),
        name="section_backward",
    )(table, incoming, gain, down, up, in_hbm(loss_grad), limits, *map(in_hbm, kept[:-1]), kept[-1])
    return got[:3], got[3:7], got[7]


def empty_buffers(shapes):
    return pl.pallas_call(
        lambda *refs: None,
        out_shape=[jax.ShapeDtypeStruct(dims, kind) for dims, kind in shapes],
        out_specs=[ANY] * len(shapes),
        name="empty_buffers",
    )()


def assemble_kernel(place, *refs):
    parts, (down, up, gain) = refs[:16], refs[16:]
    per = 2 * SHARD // BLOCK
    for number, part in enumerate(parts):
        shard = place[number]
        rows = pl.ds(pl.multiple_of(shard * SHARD, SHARD), SHARD)
        down[rows, :] = part[:SHARD, :]
        up[rows, :] = part[SHARD : 2 * SHARD, :]
        if number % 2 == 0:
            piece = part[2 * SHARD :, :BLOCK].astype(F32)
            for line in range(per):
                gain[pl.ds((shard >> 1) * per + line, 1), :] = piece[line : line + 1, :]


def assemble(place, parts):
    return pl.pallas_call(
        assemble_kernel,
        out_shape=[
            jax.ShapeDtypeStruct((WIDTH, NECK), BF16),
            jax.ShapeDtypeStruct((WIDTH, NECK), BF16),
            jax.ShapeDtypeStruct((WIDTH // BLOCK, BLOCK), F32),
        ],
        in_specs=[SM] + [VM] * 16,
        out_specs=[VM] * 3,
        compiler_params=call_params(8),
        cost_estimate=pl.CostEstimate(flops=0, bytes_accessed=19_000_000, transcendentals=0),
        name="assemble_weights",
    )(place, *parts)


def fsdp_index(y, z, core):
    return y * 4 + z * 2 + core


def fsdp_pairs(move):
    return [
        (fsdp_index(y, z, core), fsdp_index(*move(y, z, core)))
        for y in range(4)
        for z in range(2)
        for core in range(2)
    ]


def to_core(value):
    return lax.ppermute(value, "fsdp", fsdp_pairs(lambda y, z, core: (y, z, 1 - core)))


def along_z(value):
    return lax.ppermute(value, "fsdp", fsdp_pairs(lambda y, z, core: (y, 1 - z, core)))


def along_y(value, by):
    return lax.ppermute(value, "fsdp", fsdp_pairs(lambda y, z, core: ((y + by) % 4, z, core)))


def gather_parts(own, beside):
    parts = {(0, 0): own}
    parts[(0, 1)] = along_z(own)
    for by in (1, 3, 2):
        parts[(by, 0)] = along_y(own, -by)
    parts[(0, 1)], made = beside(parts[(0, 1)])
    parts[(2, 1)] = along_z(parts[(2, 0)])
    for by in (1, 3):
        parts[(by, 1)] = along_y(parts[(0, 1)], -by)
    return parts, made


def gradient_kernel(order, normed, neckcot, cot, act, gains, mine, theirs, hold):
    factor = 1.0 / math.sqrt(MICRO * TOKENS * 16)
    core = order[8]
    both = 2 * SHARD
    for number, (left, right) in enumerate(((normed, neckcot), (cot, act))):
        hold[...] = (
            lax.dot_general(left[...], right[...], TN, preferred_element_type=F32) * factor
        ).astype(BF16)
        rows = slice(number * SHARD, (number + 1) * SHARD)
        mine[0, rows, :] = hold[pl.ds(pl.multiple_of(core * SHARD, SHARD), SHARD), :]
        theirs[0, rows, :] = hold[pl.ds(pl.multiple_of((1 - core) * SHARD, SHARD), SHARD), :]
    sums = jnp.sum(gains[...], axis=0, keepdims=True) * factor
    lines = [sums[:, start : start + BLOCK] for start in range(0, both, BLOCK)]
    lines.append(jnp.zeros((EXTRA - len(lines), BLOCK), F32))
    lines = jnp.concatenate(lines, axis=0).astype(BF16)
    lines = jnp.concatenate([lines, lines], axis=1)
    mine[0, both:, :] = lines
    theirs[0, both:, :] = lines


def gradient_blocks(order, first, count, normed, neckcot, cot, act, gains):
    rows = MICRO * TOKENS
    block = pl.BlockSpec((rows, 2 * SHARD), lambda i, order: (0, order[first + i]))
    small = pl.BlockSpec((rows, NECK), lambda i, order: (0, 0))
    result = pl.BlockSpec((1, 2 * SHARD + EXTRA, NECK), lambda i, order: (i, 0, 0))
    return pl.pallas_call(
        gradient_kernel,
        grid_spec=pltpu.PrefetchScalarGridSpec(
            num_scalar_prefetch=1,
            grid=(count,),
            in_specs=[
                block,
                small,
                block,
                small,
                pl.BlockSpec((8, 2 * SHARD), lambda i, order: (0, order[first + i])),
            ],
            out_specs=[result, result],
            scratch_shapes=[pltpu.VMEM((2 * SHARD, NECK), BF16)],
        ),
        out_shape=[jax.ShapeDtypeStruct((count, 2 * SHARD + EXTRA, NECK), BF16)] * 2,
        compiler_params=call_params(8),
        name="gradient_blocks",
    )(order, in_hbm(normed), neckcot, in_hbm(cot), act, gains)


REDUCE_ORDER = ((1, 1), (3, 1), (2, 1), (1, 0), (3, 0), (2, 0), (0, 1), (0, 0))


def widen(value):
    return value.astype(F32)


def reduce_parts(order, normed, neckcot, cot, act, gains):
    blocks = {}
    for first in (0, 4):
        mine, theirs = gradient_blocks(order, first, 4, normed, neckcot, cot, act, gains)
        theirs = to_core(theirs)
        for number in range(4):
            blocks[REDUCE_ORDER[first + number]] = (mine[number], theirs[number])

    def summed(key, *others):
        mine, theirs = blocks[key]
        total = widen(mine) + widen(theirs)
        for other in others:
            total += widen(other)
        return total

    def narrow(value):
        return value.astype(BF16)

    first = along_y(narrow(summed((1, 1))), 1)
    second = along_y(narrow(summed((3, 1))), 3)
    third = along_z(narrow(summed((2, 1))))
    fourth = along_y(narrow(summed((1, 0))), 1)
    fifth = along_y(narrow(summed((3, 0))), 3)
    sixth = along_y(narrow(summed((2, 0), third)), 2)
    seventh = along_z(narrow(summed((0, 1), first, second)))
    return summed((0, 0), fourth, fifth, sixth, seventh)


def shards(
    in_base,
    out_base,
    sample_ids,
    send_exponent,
    grad_exponent,
    loss_grad,
    down_weight,
    up_weight,
    norm_gain,
):
    section = lax.axis_index("section")
    place = lax.axis_index("fsdp")
    y, z, core = place >> 2, (place >> 1) & 1, place & 1
    tokens = MICRO * TOKENS
    ticks = CHUNKS + 2 * DEPTH

    other = to_core(norm_gain)
    pair = jnp.where(
        core == 0,
        jnp.concatenate([norm_gain, other], axis=1),
        jnp.concatenate([other, norm_gain], axis=1),
    ).reshape(2 * SHARD // BLOCK, BLOCK)
    gain_rows = jnp.pad(pair, ((0, EXTRA - pair.shape[0]), (0, NECK - BLOCK)))
    own = jnp.concatenate([down_weight[0], up_weight[0], gain_rows], axis=0)
    def schedule(early):
        early, ids, sending, going_back = lax.optimization_barrier(
            (early, sample_ids, send_exponent, grad_exponent)
        )
        tick = jnp.arange(ticks, dtype=jnp.int32)

        def lane(chunk):
            active = (chunk >= 0) & (chunk < CHUNKS)
            chunk = jnp.clip(chunk, 0, CHUNKS - 1)
            return active.astype(jnp.int32), chunk

        per = TOKENS // ROWS
        ahead, chunk = lane(tick - STRIDE * section)
        base = ids[chunk // per] * TOKENS + (chunk % per) * ROWS
        back, reverse = lane(tick - 2 * DEPTH + STRIDE * section)
        last = jnp.full((ticks,), section == SECTIONS - 1).astype(jnp.int32)
        table = jnp.stack([ahead, chunk * ROWS, base, back, reverse * ROWS, last], axis=1)

        def limit(exponent):
            exponent = exponent[0].reshape(tokens, WIDTH // BLOCK)
            level = jnp.zeros(exponent.shape, F32)
            for value in range(LOWEST_EXPONENT, HIGHEST_EXPONENT):
                level = jnp.where(exponent == value, F32(CLIP_LEVEL * 2.0**value), level)
            return level

        made = (table, limit(sending), limit(going_back))
        return lax.optimization_barrier((early, made))

    parts, (table, send_limit, back_limit) = gather_parts(own, schedule)
    pieces, places = [], []
    for (dy, dz), part in parts.items():
        spot = fsdp_index((y + dy) & 3, z ^ dz, core)
        pieces += [part, to_core(part)]
        places += [spot, spot + 1 - 2 * core]
    down, up, gain = assemble(jnp.stack(places).astype(jnp.int32), pieces)

    base_in = in_base.reshape(-1, WIDTH)
    base_out = out_base.reshape(-1, WIDTH)
    loss = loss_grad.reshape(tokens, WIDTH)

    buffers = empty_buffers(
        [
            ((tokens, WIDTH), BF16),
            ((tokens, WIDTH), BF16),
            ((tokens, NECK), F32),
            ((tokens, NECK), BF16),
            ((tokens, WIDTH), BF16),
            ((tokens, 2 * BLOCK), F32),
            ((tokens, WIDTH), BF16),
            ((tokens, WIDTH), BF16),
            ((tokens, NECK), BF16),
        ]
    )
    layer, out, neck, act, normed, stat = buffers[:6]
    cots = [*buffers[6:], jnp.zeros((8, WIDTH), F32)]
    zero = jnp.zeros((ROWS, WIDTH), BF16)
    onward = [(s, s + 1) for s in range(SECTIONS - 1)]
    inverse = [(s + 1, s) for s in range(SECTIONS - 1)]
    arriving, returning = [zero] * STRIDE, [zero] * STRIDE
    for step in range(ticks):
        if step < CHUNKS + DEPTH:
            (layer, out, neck, act, normed, stat), delivered = forward_call(
                step,
                table,
                arriving.pop(0),
                gain,
                down,
                up,
                base_in,
                base_out,
                send_limit,
                (layer, out, neck, act, normed, stat),
            )
            arriving.append(lax.ppermute(delivered, "section", onward))
        if step >= DEPTH:
            (layer, neck, stat), cots, sent = backward_call(
                step,
                table,
                returning.pop(0),
                gain,
                down,
                up,
                loss,
                back_limit,
                (layer, neck, stat),
                cots,
            )
            returning.append(lax.ppermute(sent, "section", inverse))

    grad, cot, neckcot, gain_sums = cots
    order = [((y + dy) & 3) * 2 + (z ^ dz) for dy, dz in REDUCE_ORDER] + [core]
    order = jnp.stack(order).astype(jnp.int32)
    total = reduce_parts(order, normed, neckcot, cot, act, gain_sums)
    shape = (1, MICRO, TOKENS, WIDTH)
    return (
        out.reshape(shape),
        grad.reshape(shape),
        total[None, :SHARD],
        total[None, SHARD : 2 * SHARD],
        lax.dynamic_slice_in_dim(
            total[2 * SHARD : 2 * SHARD + 9, :BLOCK].reshape(1, 2 * SHARD), core * SHARD, SHARD, 1
        ),
    )


def solution(mesh):
    in_specs = (
        P("section", None, "fsdp", None),
        P("section", None, "fsdp", None),
        P(),
        P("section", None, "fsdp", None),
        P("section", None, "fsdp", None),
        P(None, "fsdp", None),
        P("section", "fsdp", None),
        P("section", "fsdp", None),
        P("section", "fsdp"),
    )
    out_specs = (
        P("section", None, "fsdp", None),
        P("section", None, "fsdp", None),
        P("section", "fsdp", None),
        P("section", "fsdp", None),
        P("section", "fsdp"),
    )
    return jax.shard_map(shards, mesh=mesh, in_specs=in_specs, out_specs=out_specs, check_vma=False)
```

```python
import functools
import math

import jax
import jax.numpy as jnp
from jax import lax
from jax.experimental import pallas as pl
from jax.experimental.pallas import tpu as pltpu
from jax.sharding import PartitionSpec as P

SQRT_HALF = 0.7071067811865476
INV_ROOT_TAU = 0.3989422804014327
CLIP_LEVEL = 448.0
NORM_EPSILON = 1e-05
LOWEST_EXPONENT = -9
HIGHEST_EXPONENT = -3

SECTIONS = 8
WIDTH = 9216
NECK = 256
BLOCK = 128
TOKENS = 48
MICRO = 4
ROWS = 16
CHUNKS = MICRO * TOKENS // ROWS
SHARD = 576
STRIDE = 2
DEPTH = STRIDE * (SECTIONS - 1)
EXTRA = 16
WIDE = 1024
MEDIUM = 512

VM = pl.BlockSpec(memory_space=pltpu.VMEM)
SM = pl.BlockSpec(memory_space=pltpu.SMEM)
ANY = pl.BlockSpec(memory_space=pltpu.HBM)
NT = (((1,), (1,)), ((), ()))
TN = (((0,), (0,)), ((), ()))
F32 = jnp.float32
BF16 = jnp.bfloat16


def in_hbm(value):
    return pltpu.with_memory_space_constraint(value, pltpu.HBM)


def lane_sum(values):
    return jnp.sum(values, axis=-1, keepdims=True)


def gain_row(gain, start, size):
    first = start // BLOCK
    rows = [gain[first + number : first + number + 1, :] for number in range(size // BLOCK)]
    return jnp.concatenate(rows, axis=1)


def clipped(values, limits, start):
    pieces = []
    for offset in range(0, values.shape[1], BLOCK):
        index = (start + offset) // BLOCK
        bound = jnp.broadcast_to(limits[:, index : index + 1], (values.shape[0], BLOCK))
        pieces.append(jnp.clip(values[:, offset : offset + BLOCK], -bound, bound))
    return jnp.concatenate(pieces, axis=1).astype(BF16)


def forward_kernel(
    tick,
    table,
    incoming,
    gain,
    down,
    up,
    base_in,
    base_out,
    limits,
    *refs,
):
    (outs, scratch) = (refs[6:13], refs[13:])
    layer_all, out_all, neck_all, act_all, normed_all, stat_all, delivered = outs
    rows_in, rows_out, bound, layer, section, neck, act, normed, stat, sems = scratch

    @pl.when(table[tick, 0] == 1)
    def _():
        row = pl.multiple_of(table[tick, 1], ROWS)
        base = pl.multiple_of(table[tick, 2], ROWS)
        here = pl.ds(row, ROWS)
        loads = [
            pltpu.make_async_copy(base_in.at[pl.ds(base, ROWS), :], rows_in, sems.at[0]),
            pltpu.make_async_copy(base_out.at[pl.ds(base, ROWS), :], rows_out, sems.at[1]),
            pltpu.make_async_copy(limits.at[here, :], bound, sems.at[2]),
        ]
        for copy in loads:
            copy.start()
        stores = [
            pltpu.make_async_copy(source, target.at[here, :], sems.at[3 + number])
            for number, (source, target) in enumerate(
                (
                    (layer, layer_all),
                    (section, out_all),
                    (neck, neck_all),
                    (act, act_all),
                    (normed, normed_all),
                    (stat, stat_all),
                )
            )
        ]
        loads[0].wait()
        total = jnp.zeros((ROWS, BLOCK), F32)
        for start in range(0, WIDTH, WIDE):
            span = slice(start, start + WIDE)
            values = (rows_in[:, span].astype(F32) + incoming[:, span].astype(F32)).astype(BF16)
            layer[:, span] = values
            values = values.astype(F32)
            for offset in range(0, WIDE, BLOCK):
                total += values[:, offset : offset + BLOCK]
        stores[0].start()
        mean = lane_sum(total) * (1.0 / WIDTH)
        total = jnp.zeros((ROWS, BLOCK), F32)
        for start in range(0, WIDTH, WIDE):
            values = layer[:, start : start + WIDE].astype(F32) - mean
            values = values * values
            for offset in range(0, WIDE, BLOCK):
                total += values[:, offset : offset + BLOCK]
        scale = lax.rsqrt(lane_sum(total) * (1.0 / WIDTH) + NORM_EPSILON)
        stat[:, :BLOCK] = jnp.broadcast_to(mean, (ROWS, BLOCK))
        stat[:, BLOCK:] = jnp.broadcast_to(scale, (ROWS, BLOCK))
        stores[5].start()
        result = jnp.zeros((ROWS, NECK), F32)
        for start in range(0, WIDTH, WIDE):
            span = slice(start, start + WIDE)
            values = (layer[:, span].astype(F32) - mean) * scale
            values = (values * gain_row(gain, start, WIDE)).astype(BF16)
            normed[:, span] = values
            result += jnp.dot(values, down[span, :], preferred_element_type=F32)
        stores[4].start()
        neck[...] = result
        stores[2].start()
        activated = (result * 0.5 * (1.0 + lax.erf(result * SQRT_HALF))).astype(BF16)
        act[...] = activated
        stores[3].start()
        loads[1].wait()
        loads[2].wait()
        edges = bound[...]
        for start in range(0, WIDTH, MEDIUM):
            span = slice(start, start + MEDIUM)
            branch = lax.dot_general(activated, up[span, :], NT, preferred_element_type=F32)
            value = (layer[:, span].astype(F32) + branch).astype(BF16)
            section[:, span] = value
            change = value.astype(F32) - rows_out[:, span].astype(F32)
            delivered[:, span] = clipped(change, edges, start)
        stores[1].start()
        for copy in stores:
            copy.wait()


def backward_kernel(
    tick,
    table,
    incoming,
    gain,
    down,
    up,
    loss_grad,
    limits,
    layer_all,
    neck_all,
    stat_all,
    *refs,
):
    (outs, scratch) = (refs[4:12], refs[12:])
    gain_before = refs[3]
    grad_all, cot_all, neckcot_all, gain_sums, sent = outs[3:]
    cot, bound, layer, neck, stat, grad, neckcot, hold, sems = scratch

    gain_sums[...] = gain_before[...]

    @pl.when(table[tick, 3] == 1)
    def _():
        row = pl.multiple_of(table[tick, 4], ROWS)
        here = pl.ds(row, ROWS)
        last = table[tick, 5] == 1
        loads = [
            pltpu.make_async_copy(limits.at[here, :], bound, sems.at[0]),
            pltpu.make_async_copy(layer_all.at[here, :], layer, sems.at[1]),
            pltpu.make_async_copy(neck_all.at[here, :], neck, sems.at[2]),
            pltpu.make_async_copy(stat_all.at[here, :], stat, sems.at[3]),
        ]
        for copy in loads:
            copy.start()
        stores = [
            pltpu.make_async_copy(grad, grad_all.at[here, :], sems.at[4]),
            pltpu.make_async_copy(cot, cot_all.at[here, :], sems.at[5]),
            pltpu.make_async_copy(neckcot, neckcot_all.at[here, :], sems.at[6]),
        ]

        @pl.when(last)
        def _():
            fetch = pltpu.make_async_copy(loss_grad.at[here, :], cot, sems.at[8])
            fetch.start()
            fetch.wait()

        @pl.when(jnp.logical_not(last))
        def _():
            cot[...] = incoming[...]

        stores[1].start()
        result = jnp.zeros((ROWS, NECK), F32)
        for start in range(0, WIDTH, WIDE):
            span = slice(start, start + WIDE)
            result += jnp.dot(cot[:, span], up[span, :], preferred_element_type=F32)
        loads[2].wait()
        bottle = neck[...]
        slope = 0.5 * (1.0 + lax.erf(bottle * SQRT_HALF)) + bottle * INV_ROOT_TAU * jnp.exp(
            -0.5 * bottle * bottle
        )
        small = (result * slope).astype(BF16)
        neckcot[...] = small
        stores[2].start()
        loads[1].wait()
        loads[3].wait()
        mean = stat[:, :1]
        scale = stat[:, BLOCK : BLOCK + 1]
        first = jnp.zeros((ROWS, BLOCK), F32)
        second = jnp.zeros((ROWS, BLOCK), F32)
        for start in range(0, WIDTH, MEDIUM):
            span = slice(start, start + MEDIUM)
            wide = lax.dot_general(small, down[span, :], NT, preferred_element_type=F32)
            centred = (layer[:, span].astype(F32) - mean) * scale
            product = wide * centred
            gain_sums[:, span] += product[:8, :] + product[8:, :]
            scaled = wide * gain_row(gain, start, MEDIUM)
            hold[:, span] = scaled
            product = scaled * centred
            for offset in range(0, MEDIUM, BLOCK):
                first += scaled[:, offset : offset + BLOCK]
                second += product[:, offset : offset + BLOCK]
        first = lane_sum(first) * (1.0 / WIDTH)
        second = lane_sum(second) * (1.0 / WIDTH)
        loads[0].wait()
        edges = bound[...]
        for start in range(0, WIDTH, MEDIUM):
            span = slice(start, start + MEDIUM)
            centred = (layer[:, span].astype(F32) - mean) * scale
            value = cot[:, span].astype(F32) + scale * (hold[:, span] - first - centred * second)
            grad[:, span] = value.astype(BF16)
            sent[:, span] = clipped(value, edges, start)
        stores[0].start()
        for copy in stores:
            copy.wait()


def call_params(megabytes):
    return pltpu.CompilerParams(vmem_limit_bytes=megabytes << 20)


def forward_call(tick, table, incoming, gain, down, up, base_in, base_out, limits, state):
    shape = jax.ShapeDtypeStruct
    outs = [shape(item.shape, item.dtype) for item in state] + [shape((ROWS, WIDTH), BF16)]
    held = [item if number == 1 else in_hbm(item) for number, item in enumerate(state)]
    got = pl.pallas_call(
        functools.partial(forward_kernel, tick),
        out_shape=outs,
        in_specs=[SM, VM, VM, VM, VM, ANY, ANY, ANY] + [ANY] * 6,
        out_specs=[ANY] * 6 + [VM],
        scratch_shapes=[
            pltpu.VMEM((ROWS, WIDTH), BF16),
            pltpu.VMEM((ROWS, WIDTH), BF16),
            pltpu.VMEM((ROWS, WIDTH // BLOCK), F32),
            pltpu.VMEM((ROWS, WIDTH), BF16),
            pltpu.VMEM((ROWS, WIDTH), BF16),
            pltpu.VMEM((ROWS, NECK), F32),
            pltpu.VMEM((ROWS, NECK), BF16),
            pltpu.VMEM((ROWS, WIDTH), BF16),
            pltpu.VMEM((ROWS, 2 * BLOCK), F32),
            pltpu.SemaphoreType.DMA((9,)),
        ],
        input_output_aliases={8 + number: number for number in range(6)},
        compiler_params=call_params(8),
        cost_estimate=pl.CostEstimate(flops=150_000_000, bytes_accessed=9_000_000, transcendentals=0),
        name="section_forward",
    )(table, incoming, gain, down, up, base_in, base_out, limits, *held)
    return got[:6], got[6]


def backward_call(tick, table, incoming, gain, down, up, loss_grad, limits, saved, state):
    shape = jax.ShapeDtypeStruct
    kept = list(saved) + list(state)
    outs = [shape(item.shape, item.dtype) for item in kept] + [shape((ROWS, WIDTH), BF16)]
    got = pl.pallas_call(
        functools.partial(backward_kernel, tick),
        out_shape=outs,
        in_specs=[SM, VM, VM, VM, VM, ANY, ANY] + [ANY] * 6 + [VM],
        out_specs=[ANY] * 6 + [VM, VM],
        scratch_shapes=[
            pltpu.VMEM((ROWS, WIDTH), BF16),
            pltpu.VMEM((ROWS, WIDTH // BLOCK), F32),
            pltpu.VMEM((ROWS, WIDTH), BF16),
            pltpu.VMEM((ROWS, NECK), F32),
            pltpu.VMEM((ROWS, 2 * BLOCK), F32),
            pltpu.VMEM((ROWS, WIDTH), BF16),
            pltpu.VMEM((ROWS, NECK), BF16),
            pltpu.VMEM((ROWS, WIDTH), F32),
            pltpu.SemaphoreType.DMA((9,)),
        ],
        input_output_aliases={7 + number: number for number in range(7)},
        compiler_params=call_params(8),
        cost_estimate=pl.CostEstimate(flops=150_000_000, bytes_accessed=9_000_000, transcendentals=0),
        name="section_backward",
    )(table, incoming, gain, down, up, in_hbm(loss_grad), limits, *map(in_hbm, kept[:-1]), kept[-1])
    return got[:3], got[3:7], got[7]


def empty_buffers(shapes):
    return pl.pallas_call(
        lambda *refs: None,
        out_shape=[jax.ShapeDtypeStruct(dims, kind) for dims, kind in shapes],
        out_specs=[ANY] * len(shapes),
        name="empty_buffers",
    )()


def assemble_kernel(place, *refs):
    parts, (down, up, gain) = refs[:16], refs[16:]
    per = 2 * SHARD // BLOCK
    for number, part in enumerate(parts):
        shard = place[number]
        rows = pl.ds(pl.multiple_of(shard * SHARD, SHARD), SHARD)
        down[rows, :] = part[:SHARD, :]
        up[rows, :] = part[SHARD : 2 * SHARD, :]
        if number % 2 == 0:
            piece = part[2 * SHARD :, :BLOCK].astype(F32)
            for line in range(per):
                gain[pl.ds((shard >> 1) * per + line, 1), :] = piece[line : line + 1, :]


def assemble(place, parts):
    return pl.pallas_call(
        assemble_kernel,
        out_shape=[
            jax.ShapeDtypeStruct((WIDTH, NECK), BF16),
            jax.ShapeDtypeStruct((WIDTH, NECK), BF16),
            jax.ShapeDtypeStruct((WIDTH // BLOCK, BLOCK), F32),
        ],
        in_specs=[SM] + [VM] * 16,
        out_specs=[VM] * 3,
        compiler_params=call_params(8),
        cost_estimate=pl.CostEstimate(flops=0, bytes_accessed=19_000_000, transcendentals=0),
        name="assemble_weights",
    )(place, *parts)


def fsdp_index(y, z, core):
    return y * 4 + z * 2 + core


def fsdp_pairs(move):
    return [
        (fsdp_index(y, z, core), fsdp_index(*move(y, z, core)))
        for y in range(4)
        for z in range(2)
        for core in range(2)
    ]


def to_core(value):
    return lax.ppermute(value, "fsdp", fsdp_pairs(lambda y, z, core: (y, z, 1 - core)))


def along_z(value):
    return lax.ppermute(value, "fsdp", fsdp_pairs(lambda y, z, core: (y, 1 - z, core)))


def along_y(value, by):
    return lax.ppermute(value, "fsdp", fsdp_pairs(lambda y, z, core: ((y + by) % 4, z, core)))


def gather_parts(own, beside):
    parts = {(0, 0): own}
    parts[(0, 1)] = along_z(own)
    for by in (1, 3, 2):
        parts[(by, 0)] = along_y(own, -by)
    parts[(0, 1)], made = beside(parts[(0, 1)])
    parts[(2, 1)] = along_z(parts[(2, 0)])
    for by in (1, 3):
        parts[(by, 1)] = along_y(parts[(0, 1)], -by)
    return parts, made


def gradient_kernel(order, normed, neckcot, cot, act, gains, mine, theirs, hold):
    factor = 1.0 / math.sqrt(MICRO * TOKENS * 16)
    core = order[8]
    both = 2 * SHARD
    for number, (left, right) in enumerate(((normed, neckcot), (cot, act))):
        hold[...] = (
            lax.dot_general(left[...], right[...], TN, preferred_element_type=F32) * factor
        ).astype(BF16)
        rows = slice(number * SHARD, (number + 1) * SHARD)
        mine[0, rows, :] = hold[pl.ds(pl.multiple_of(core * SHARD, SHARD), SHARD), :]
        theirs[0, rows, :] = hold[pl.ds(pl.multiple_of((1 - core) * SHARD, SHARD), SHARD), :]
    sums = jnp.sum(gains[...], axis=0, keepdims=True) * factor
    lines = [sums[:, start : start + BLOCK] for start in range(0, both, BLOCK)]
    lines.append(jnp.zeros((EXTRA - len(lines), BLOCK), F32))
    lines = jnp.concatenate(lines, axis=0).astype(BF16)
    lines = jnp.concatenate([lines, lines], axis=1)
    mine[0, both:, :] = lines
    theirs[0, both:, :] = lines


def gradient_blocks(order, first, count, normed, neckcot, cot, act, gains):
    rows = MICRO * TOKENS
    block = pl.BlockSpec((rows, 2 * SHARD), lambda i, order: (0, order[first + i]))
    small = pl.BlockSpec((rows, NECK), lambda i, order: (0, 0))
    result = pl.BlockSpec((1, 2 * SHARD + EXTRA, NECK), lambda i, order: (i, 0, 0))
    return pl.pallas_call(
        gradient_kernel,
        grid_spec=pltpu.PrefetchScalarGridSpec(
            num_scalar_prefetch=1,
            grid=(count,),
            in_specs=[
                block,
                small,
                block,
                small,
                pl.BlockSpec((8, 2 * SHARD), lambda i, order: (0, order[first + i])),
            ],
            out_specs=[result, result],
            scratch_shapes=[pltpu.VMEM((2 * SHARD, NECK), BF16)],
        ),
        out_shape=[jax.ShapeDtypeStruct((count, 2 * SHARD + EXTRA, NECK), BF16)] * 2,
        compiler_params=call_params(8),
        name="gradient_blocks",
    )(order, in_hbm(normed), neckcot, in_hbm(cot), act, gains)


REDUCE_ORDER = ((1, 1), (3, 1), (2, 1), (1, 0), (3, 0), (2, 0), (0, 1), (0, 0))


def widen(value):
    return value.astype(F32)


def reduce_parts(order, normed, neckcot, cot, act, gains):
    blocks = {}
    for first in (0, 4):
        mine, theirs = gradient_blocks(order, first, 4, normed, neckcot, cot, act, gains)
        theirs = to_core(theirs)
        for number in range(4):
            blocks[REDUCE_ORDER[first + number]] = (mine[number], theirs[number])

    def summed(key, *others):
        mine, theirs = blocks[key]
        total = widen(mine) + widen(theirs)
        for other in others:
            total += widen(other)
        return total

    def narrow(value):
        return value.astype(BF16)

    first = along_y(narrow(summed((1, 1))), 1)
    second = along_y(narrow(summed((3, 1))), 3)
    third = along_z(narrow(summed((2, 1))))
    fourth = along_y(narrow(summed((1, 0))), 1)
    fifth = along_y(narrow(summed((3, 0))), 3)
    sixth = along_y(narrow(summed((2, 0), third)), 2)
    seventh = along_z(narrow(summed((0, 1), first, second)))
    return summed((0, 0), fourth, fifth, sixth, seventh)


def shards(
    in_base,
    out_base,
    sample_ids,
    send_exponent,
    grad_exponent,
    loss_grad,
    down_weight,
    up_weight,
    norm_gain,
):
    section = lax.axis_index("section")
    place = lax.axis_index("fsdp")
    y, z, core = place >> 2, (place >> 1) & 1, place & 1
    tokens = MICRO * TOKENS
    ticks = CHUNKS + 2 * DEPTH

    other = to_core(norm_gain)
    pair = jnp.where(
        core == 0,
        jnp.concatenate([norm_gain, other], axis=1),
        jnp.concatenate([other, norm_gain], axis=1),
    ).reshape(2 * SHARD // BLOCK, BLOCK)
    gain_rows = jnp.pad(pair, ((0, EXTRA - pair.shape[0]), (0, NECK - BLOCK)))
    own = jnp.concatenate([down_weight[0], up_weight[0], gain_rows], axis=0)
    def schedule(early):
        early, ids, sending, going_back = lax.optimization_barrier(
            (early, sample_ids, send_exponent, grad_exponent)
        )
        tick = jnp.arange(ticks, dtype=jnp.int32)

        def lane(chunk):
            active = (chunk >= 0) & (chunk < CHUNKS)
            chunk = jnp.clip(chunk, 0, CHUNKS - 1)
            return active.astype(jnp.int32), chunk

        per = TOKENS // ROWS
        ahead, chunk = lane(tick - STRIDE * section)
        base = ids[chunk // per] * TOKENS + (chunk % per) * ROWS
        back, reverse = lane(tick - 2 * DEPTH + STRIDE * section)
        last = jnp.full((ticks,), section == SECTIONS - 1).astype(jnp.int32)
        table = jnp.stack([ahead, chunk * ROWS, base, back, reverse * ROWS, last], axis=1)

        def limit(exponent):
            exponent = exponent[0].reshape(tokens, WIDTH // BLOCK)
            level = jnp.zeros(exponent.shape, F32)
            for value in range(LOWEST_EXPONENT, HIGHEST_EXPONENT):
                level = jnp.where(exponent == value, F32(CLIP_LEVEL * 2.0**value), level)
            return level

        made = (table, limit(sending), limit(going_back))
        return lax.optimization_barrier((early, made))

    parts, (table, send_limit, back_limit) = gather_parts(own, schedule)
    pieces, places = [], []
    for (dy, dz), part in parts.items():
        spot = fsdp_index((y + dy) & 3, z ^ dz, core)
        pieces += [part, to_core(part)]
        places += [spot, spot + 1 - 2 * core]
    down, up, gain = assemble(jnp.stack(places).astype(jnp.int32), pieces)

    base_in = in_base.reshape(-1, WIDTH)
    base_out = out_base.reshape(-1, WIDTH)
    loss = loss_grad.reshape(tokens, WIDTH)

    buffers = empty_buffers(
        [
            ((tokens, WIDTH), BF16),
            ((tokens, WIDTH), BF16),
            ((tokens, NECK), F32),
            ((tokens, NECK), BF16),
            ((tokens, WIDTH), BF16),
            ((tokens, 2 * BLOCK), F32),
            ((tokens, WIDTH), BF16),
            ((tokens, WIDTH), BF16),
            ((tokens, NECK), BF16),
        ]
    )
    layer, out, neck, act, normed, stat = buffers[:6]
    cots = [*buffers[6:], jnp.zeros((8, WIDTH), F32)]
    zero = jnp.zeros((ROWS, WIDTH), BF16)
    onward = [(s, s + 1) for s in range(SECTIONS - 1)]
    inverse = [(s + 1, s) for s in range(SECTIONS - 1)]
    arriving, returning = [zero] * STRIDE, [zero] * STRIDE
    for step in range(ticks):
        if step < CHUNKS + DEPTH:
            (layer, out, neck, act, normed, stat), delivered = forward_call(
                step,
                table,
                arriving.pop(0),
                gain,
                down,
                up,
                base_in,
                base_out,
                send_limit,
                (layer, out, neck, act, normed, stat),
            )
            arriving.append(lax.ppermute(delivered, "section", onward))
        if step >= DEPTH:
            (layer, neck, stat), cots, sent = backward_call(
                step,
                table,
                returning.pop(0),
                gain,
                down,
                up,
                loss,
                back_limit,
                (layer, neck, stat),
                cots,
            )
            returning.append(lax.ppermute(sent, "section", inverse))

    grad, cot, neckcot, gain_sums = cots
    order = [((y + dy) & 3) * 2 + (z ^ dz) for dy, dz in REDUCE_ORDER] + [core]
    order = jnp.stack(order).astype(jnp.int32)
    total = reduce_parts(order, normed, neckcot, cot, act, gain_sums)
    shape = (1, MICRO, TOKENS, WIDTH)
    return (
        out.reshape(shape),
        grad.reshape(shape),
        total[None, :SHARD],
        total[None, SHARD : 2 * SHARD],
        lax.dynamic_slice_in_dim(
            total[2 * SHARD : 2 * SHARD + 9, :BLOCK].reshape(1, 2 * SHARD), core * SHARD, SHARD, 1
        ),
    )


def solution(mesh):
    in_specs = (
        P("section", None, "fsdp", None),
        P("section", None, "fsdp", None),
        P(),
        P("section", None, "fsdp", None),
        P("section", None, "fsdp", None),
        P(None, "fsdp", None),
        P("section", "fsdp", None),
        P("section", "fsdp", None),
        P("section", "fsdp"),
    )
    out_specs = (
        P("section", None, "fsdp", None),
        P("section", None, "fsdp", None),
        P("section", "fsdp", None),
        P("section", "fsdp", None),
        P("section", "fsdp"),
    )
    return jax.shard_map(shards, mesh=mesh, in_specs=in_specs, out_specs=out_specs, check_vma=False)
```
